128 devices in a mesh: smp: 8 (over y, z_lo), par: 16 (over x, z_hi, core).
Axes of the slice: x: 4, y: 4, z: 4 (z_hi: 2, z_lo: 2; z = z_hi * 2 + z_lo), core: 2. Of those that a mesh axis runs over, the one named last changes fastest.
Arguments:
- log_derivs: bfloat16 [2048, 65536], P('smp', 'par')
- spins: int32 [2048, 100], P('smp'), may hold values from 0 to 1
- hop_energy: float32 [2048], P('smp'), may hold values from -8 to 8
Outputs:
- update: float32 [65536], P('par')
- coeffs: float32 [2048], P('smp')
The draws below stay inside these ranges and needn't reach their ends.
All inputs are finite; a program needn't handle non-finite values.
Results may differ from the reference program's by a relative error of at most 0.0091.
The reference program's roundings to bfloat16 on the way (of `centered`) count: a program that leaves them out, or rounds other values in their place, can miss the bound.
Values may be sent and summed in bfloat16 or wider, within the bound.
A program may use at most 192 MiB of HBM per device.

```python
import jax
import jax.numpy as jnp
from jax import lax

NP = 65536
SIDE = 10
SITES = 100
NS = 2048


def draw_log_derivs(key, part):
    key = jax.random.fold_in(key, 11)
    key_col, key_row, key_val, key_mean, key_order, key_amp, key_level = jax.random.split(key, 7)
    col_scale = jnp.exp(jax.random.uniform(key_col, (NP,), jnp.float32, -1.2, 1.2))
    position = jnp.arange(NS, dtype=jnp.float32)[:, None] / NS
    row_scale = (1.0 + 2.0 * position) * jnp.exp(jax.random.uniform(key_row, (NS, 1), jnp.float32, -0.35, 0.35))
    order = jax.random.permutation(key_order, NS).astype(jnp.int32)
    depth = max(NS.bit_length() - 3, 1)
    own_amp = jnp.exp(jax.random.uniform(key_amp, (NS, 1), jnp.float32, -1.0, 1.0))
    fresh = jnp.clip(jax.random.normal(key_val, (NS, NP), jnp.float32), -5.0, 5.0)
    offset = 0.3 * jax.random.normal(key_mean, (NP,), jnp.float32)
    values = 0.35 * own_amp * fresh
    for level in range(1, depth + 1):
        count = NS >> level
        level_key = jax.random.fold_in(key_level, level)
        key_base, key_group = jax.random.split(level_key, 2)
        group_amp = jnp.exp(jax.random.uniform(key_group, (count, 1), jnp.float32, -1.0, 1.0))
        base = jnp.clip(jax.random.normal(key_base, (count, NP), jnp.float32), -5.0, 5.0)
        base = base * group_amp
        values = values + 0.3 * base[jnp.right_shift(order, level)]
    return (0.1 * col_scale * (offset + values * row_scale)).astype(jnp.bfloat16)


def touch_ends(array, key, smallest, high):
    shape = array.shape
    place = [jax.random.randint(jax.random.fold_in(key, axis), (), 0, shape[axis]) for axis in range(len(shape))]
    array = array.at[tuple(place)].set(smallest)
    longest = shape.index(max(shape))
    place[longest] = (place[longest] + 1) % shape[longest]
    return array.at[tuple(place)].set(high)


def block_levels(own_key, extent, cuts, smallest, high):
    def one(dim, blocks):
        draws = jax.random.uniform(jax.random.fold_in(jax.random.fold_in(own_key, 6), dim), (blocks,), jnp.float32, smallest / len(cuts), high / len(cuts))
        return jnp.repeat(jnp.exp(draws), extent[dim] // blocks).reshape((-1,) + (1,) * (len(extent) - dim - 1))

    loudness = one(*cuts[0])
    for cut in cuts[1:]:
        loudness = loudness * one(*cut)
    return loudness


def noise(stream_key, dims, scale, most, cuts=(), kind=jnp.bfloat16):
    values = jax.random.normal(stream_key, dims, jnp.float32) * scale
    if len(cuts) > 0:
        values = block_levels(stream_key, dims, cuts, -0.22, 0.18) * values
    return jnp.clip(values, min=-most, max=most).astype(kind)


def setup_inputs(seed: int = 0) -> dict:
    seeds = jax.random.split(jax.random.key(seed), 4)
    log_derivs = draw_log_derivs(jax.random.fold_in(seeds[3], 71), 0)
    spins = touch_ends(jax.random.randint(seeds[1], (NS, SITES), 0, 2), jax.random.fold_in(seeds[1], 1), 0, 1).astype(jnp.int32)
    hop_energy = noise(seeds[2], (NS,), 2.0, 8.0, ((0, 8),), jnp.float32)
    return {"log_derivs": log_derivs, "spins": spins, "hop_energy": hop_energy}


def local_energy(spins):
    sigma = (2 * spins - 1).astype(jnp.float32).reshape(-1, SIDE, SIDE)
    right = jnp.roll(sigma, 1, axis=2)
    below = jnp.roll(sigma, 1, axis=1)
    diag_one = jnp.roll(below, 1, axis=2)
    diag_two = jnp.roll(below, -1, axis=2)
    nearest = lax.optimization_barrier(jnp.sum(sigma * right + sigma * below, axis=(1, 2)))
    second = lax.optimization_barrier(jnp.sum(sigma * diag_one + sigma * diag_two, axis=(1, 2)))
    return 0.25 * nearest + 0.125 * second

def reference(log_derivs, spins, hop_energy):
    energy = local_energy(spins) + hop_energy
    scale = 1.0 / jnp.sqrt(jnp.float32(NS))
    eps = (energy - jnp.mean(energy)) * scale
    col_mean = lax.optimization_barrier(jnp.sum(log_derivs.astype(jnp.float32), axis=0)) / NS
    centered = ((log_derivs.astype(jnp.float32) - col_mean) * scale).astype(jnp.bfloat16)
    width = 4096 if NP % 4096 == 0 else NP
    blocks = centered.reshape(NS, NP // width, width).transpose(1, 0, 2)

    def add_block(total, block):
        wide = block.astype(jnp.float32)
        return (total + jnp.dot(wide, wide.T, precision=lax.Precision.HIGHEST), None)
    gram, unused = lax.scan(add_block, jnp.zeros((NS, NS), jnp.float32), blocks)
    system = gram + 0.2 * jnp.eye(NS, dtype=jnp.float32)
    factor = jnp.linalg.cholesky(system)
    coeffs = jax.scipy.linalg.cho_solve((factor, True), eps)

    def project(block):
        return jnp.dot(coeffs, block.astype(jnp.float32), precision=lax.Precision.HIGHEST)
    update = lax.map(project, blocks).reshape(NP)
    return (update, coeffs)
```

```python
import functools
import jax, jax.numpy as jnp
from jax import lax
from jax.experimental import pallas as pl
from jax.experimental.pallas import tpu as pltpu
from jax.sharding import PartitionSpec as P

B = 256
H = 128


def split(x):
    hi = x.astype(jnp.bfloat16)
    return hi, (x - hi.astype(jnp.float32)).astype(jnp.bfloat16)


def dot3(ah, al, bh, bl, dims):
    d = lambda a, b: lax.dot_general(a, b, (dims, ((), ())), preferred_element_type=jnp.float32)
    return d(ah, bh) + (d(ah, bl) + d(al, bh))


NT = ((1,), (1,))
NN = ((1,), (0,))


def mm(a, b, dims):
    return dot3(*split(a), *split(b), dims)


def recip(x):
    r = pl.reciprocal(x, approx=True)
    return r * (2.0 - x * r)


def factor_inverse(S, T, R):
    lane = lax.broadcasted_iota(jnp.int32, (8, H), 1)
    sub = lax.broadcasted_iota(jnp.int32, (8, H), 0)
    out = []
    groups = list(S)
    for p in range(16):
        rows = groups[p]
        lo = 8 * p
        for j in range(8):
            T[8 * j : 8 * j + 8, :] = jnp.broadcast_to(rows[:, lo + j : lo + j + 1], (8, H))
        indiag = (lane >= lo) & (lane < lo + 8)
        Pi = jnp.where(indiag, (lane - lo == sub).astype(jnp.float32), rows)
        R[...] = Pi
        e = {}
        for j in range(8):
            for i in range(j, 8):
                e[i, j] = jnp.broadcast_to(T[8 * j + i : 8 * j + i + 1, :], (8, H))
        Y = [jnp.broadcast_to(R[i : i + 1, :], (8, H)) for i in range(8)]
        m, r, U = {}, [], None
        for k in range(8):
            rk = recip(e[k, k])
            r.append(rk)
            for i in range(k + 1, 8):
                m[i, k] = e[i, k] * rk
            for i in range(k + 1, 8):
                for q in range(k + 1, i + 1):
                    e[i, q] = e[i, q] - m[i, k] * e[q, k]
            for i in range(k + 1, 8):
                Y[i] = Y[i] - m[i, k] * Y[k]
            Uk = Y[k] * lax.rsqrt(e[k, k])
            U = Uk if k == 0 else jnp.where(sub == k, Uk, U)
        out.append(U)
        V = [None] * 8
        for j in range(7, -1, -1):
            v = r[j] * Y[j]
            for k in range(7, j, -1):
                v = v - m[k, j] * V[k]
            V[j] = v
        for g in range(p + 1, 16):
            old = groups[g]
            base = jnp.where(indiag, 0.0, old)
            terms = [jnp.broadcast_to(old[:, lo + j : lo + j + 1], (8, H)) * V[j] for j in range(8)]
            t = ((terms[0] + terms[1]) + (terms[2] + terms[3])) + ((terms[4] + terms[5]) + (terms[6] + terms[7]))
            groups[g] = base - t
    return out


def inverse_block(D, Wref, T, R):
    U = factor_inverse([D[8 * g : 8 * g + 8, :] for g in range(16)], T, R)
    lane = lax.broadcasted_iota(jnp.int32, (8, H), 1)
    sub = lax.broadcasted_iota(jnp.int32, (8, H), 0)
    for g in range(16):
        Wref[8 * g : 8 * g + 8, :] = jnp.where(lane <= sub + 8 * g, U[g], 0.0)


def kernel(n, a_ref, e_ref, x_ref, lhi, llo, c, ec, whi, wlo, D, W, T, R, z):
    nb = n // B

    def inner(k, _):
        rows_k = pl.ds(pl.multiple_of(k * B, B), B)
        for kk in range(nb):
            @pl.when(k == kk)
            def _():
                cols = slice(kk * B, kk * B + B)
                w = kk * B
                if kk == 0:
                    c[...] = a_ref[:, cols]
                    ec[...] = e_ref[:, cols]
                else:
                    bh, bl = lhi[w : w + B, :w], llo[w : w + B, :w]
                    eh, el = lhi[n : n + 16, :w], llo[n : n + 16, :w]
                    ec[...] = e_ref[:, cols] - dot3(eh, el, bh, bl, NT)

                    @pl.loop(kk, nb)
                    def _(i):
                        ri = pl.ds(pl.multiple_of(i * B, B), B)
                        c[ri, :] = a_ref[ri, cols] - dot3(lhi[ri, :w], llo[ri, :w], bh, bl, NT)

        d0 = pl.multiple_of(k * B, B)
        D[0] = c[pl.ds(d0, H), 0:H]
        inverse_block_ref(D, W, T, R, 0)
        c21 = c[pl.ds(d0 + H, H), 0:H]
        W1 = W[0]
        l21 = mm(c21, W1, NT)
        D[1] = c[pl.ds(d0 + H, H), H:B] - mm(l21, l21, NT)
        inverse_block_ref(D, W, T, R, 1)
        W2 = W[1]
        w21 = -mm(W2, mm(l21, W1, NN), NN)
        zero = jnp.zeros((H, H), jnp.float32)
        full = jnp.concatenate(
            [jnp.concatenate([W1, zero], 1), jnp.concatenate([w21, W2], 1)], 0
        )
        wh, wl = split(full)
        whi[k], wlo[k] = wh, wl
        for kk in range(nb):
            @pl.when(k == kk)
            def _():
                cols = slice(kk * B, kk * B + B)

                @pl.loop(kk + 1, nb)
                def _(i):
                    ri = pl.ds(pl.multiple_of(i * B, B), B)
                    ch, cl = split(c[ri, :])
                    lhi[ri, cols], llo[ri, cols] = split(dot3(ch, cl, wh, wl, NT))

                eh, el = split(ec[...])
                y = dot3(eh, el, wh, wl, NT)
                lhi[n : n + 16, cols], llo[n : n + 16, cols] = split(y)
                z[:, cols] = y
        return 0

    lax.fori_loop(0, nb, inner, 0)
    for kk in range(nb - 1, -1, -1):
        cols = slice(kk * B, kk * B + B)
        zh, zl = split(z[:, cols])
        x = dot3(zh, zl, whi[kk], wlo[kk], NN)
        x_ref[:, cols] = x
        if kk > 0:
            xh, xl = split(x)
            z[:, : kk * B] -= dot3(xh, xl, lhi[cols, : kk * B], llo[cols, : kk * B], NN)


def inverse_block_ref(D, W, T, R, h):
    inverse_block(D[h], W.at[h], T, R)


def solve(a, eps):
    n = a.shape[0]
    e = jnp.zeros((16, n), jnp.float32).at[0].set(eps)
    nb = n // B
    vm = pl.BlockSpec(memory_space=pltpu.VMEM)
    x = pl.pallas_call(
        functools.partial(kernel, n),
        out_shape=jax.ShapeDtypeStruct((16, n), jnp.float32),
        in_specs=[vm, vm],
        out_specs=vm,
        scratch_shapes=[
            pltpu.VMEM((n + 16, n), jnp.bfloat16),
            pltpu.VMEM((n + 16, n), jnp.bfloat16),
            pltpu.VMEM((n, B), jnp.float32),
            pltpu.VMEM((16, B), jnp.float32),
            pltpu.VMEM((nb, B, B), jnp.bfloat16),
            pltpu.VMEM((nb, B, B), jnp.bfloat16),
            pltpu.VMEM((2, H, H), jnp.float32),
            pltpu.VMEM((2, H, H), jnp.float32),
            pltpu.VMEM((64, H), jnp.float32),
            pltpu.VMEM((8, H), jnp.float32),
            pltpu.VMEM((16, n), jnp.float32),
        ],
        compiler_params=pltpu.CompilerParams(vmem_limit_bytes=60 * 2**20),
    )(a, e)
    return x[0]


SIDE = 10


def local_energy(spins):
    sigma = (2 * spins - 1).astype(jnp.float32).reshape(-1, SIDE, SIDE)
    right = jnp.roll(sigma, 1, axis=2)
    below = jnp.roll(sigma, 1, axis=1)
    diag_one = jnp.roll(below, 1, axis=2)
    diag_two = jnp.roll(below, -1, axis=2)
    nearest = jnp.sum(sigma * right + sigma * below, axis=(1, 2))
    second = jnp.sum(sigma * diag_one + sigma * diag_two, axis=(1, 2))
    return 0.25 * nearest + 0.125 * second


def body(log_derivs, spins, hop_energy):
    rows = log_derivs.shape[0]
    total = rows * lax.axis_size("smp")
    scale = 1.0 / jnp.sqrt(jnp.float32(total))
    energy = local_energy(spins) + hop_energy
    all_energy = lax.all_gather(energy, "smp", axis=0, tiled=True)
    eps = (all_energy - jnp.mean(all_energy)) * scale
    mine = lax.all_to_all(log_derivs, "smp", split_axis=1, concat_axis=0, tiled=True)
    wide = mine.astype(jnp.float32)
    centered = ((wide - jnp.sum(wide, axis=0) / total) * scale).astype(jnp.bfloat16)
    part = lax.dot_general(centered, centered, (NT, ((), ())), preferred_element_type=jnp.float32)
    block = lax.psum_scatter(part, ("smp", "par"), scatter_dimension=0, tiled=True)
    gram = lax.all_gather(block, ("smp", "par"), axis=0, tiled=True)
    coeffs = solve(gram + 0.2 * jnp.eye(total, dtype=jnp.float32), eps)
    term = jnp.dot(coeffs[None], centered.astype(jnp.float32), precision=lax.Precision.HIGHEST)[0]
    update = lax.all_gather(term, "smp", axis=0, tiled=True)
    start = lax.axis_index("smp") * rows
    return update, lax.dynamic_slice_in_dim(coeffs, start, rows, 0)


def solution(mesh):
    placed = (P("smp", "par"), P("smp", None), P("smp"))
    return jax.shard_map(
        body, mesh=mesh, in_specs=placed, out_specs=(P("par"), P("smp")), check_vma=False
    )
```

```python
import functools
import jax, jax.numpy as jnp
import numpy as np
from jax import lax
from jax.experimental import pallas as pl
from jax.experimental.pallas import tpu as pltpu
from jax.sharding import PartitionSpec as P

B = 256
H = 128


def split(x):
    hi = x.astype(jnp.bfloat16)
    return hi, (x - hi.astype(jnp.float32)).astype(jnp.bfloat16)


def dot3(ah, al, bh, bl, dims):
    d = lambda a, b: lax.dot_general(a, b, (dims, ((), ())), preferred_element_type=jnp.float32)
    return d(ah, bh) + (d(ah, bl) + d(al, bh))


NT = ((1,), (1,))
NN = ((1,), (0,))


def mm(a, b, dims):
    return dot3(*split(a), *split(b), dims)


def recip(x):
    r = pl.reciprocal(x, approx=True)
    return r * (2.0 - x * r)


def factor_inverse(S, T, R):
    lane = lax.broadcasted_iota(jnp.int32, (8, H), 1)
    sub = lax.broadcasted_iota(jnp.int32, (8, H), 0)
    out = []
    groups = list(S)
    for p in range(16):
        rows = groups[p]
        lo = 8 * p
        for j in range(8):
            T[8 * j : 8 * j + 8, :] = jnp.broadcast_to(rows[:, lo + j : lo + j + 1], (8, H))
        indiag = (lane >= lo) & (lane < lo + 8)
        Pi = jnp.where(indiag, (lane - lo == sub).astype(jnp.float32), rows)
        R[...] = Pi
        e = {}
        for j in range(8):
            for i in range(j, 8):
                e[i, j] = jnp.broadcast_to(T[8 * j + i : 8 * j + i + 1, :], (8, H))
        Y = [jnp.broadcast_to(R[i : i + 1, :], (8, H)) for i in range(8)]
        m, r, U = {}, [], None
        for k in range(8):
            rk = recip(e[k, k])
            r.append(rk)
            for i in range(k + 1, 8):
                m[i, k] = e[i, k] * rk
            for i in range(k + 1, 8):
                for q in range(k + 1, i + 1):
                    e[i, q] = e[i, q] - m[i, k] * e[q, k]
            for i in range(k + 1, 8):
                Y[i] = Y[i] - m[i, k] * Y[k]
            Uk = Y[k] * lax.rsqrt(e[k, k])
            U = Uk if k == 0 else jnp.where(sub == k, Uk, U)
        out.append(U)
        V = [None] * 8
        for j in range(7, -1, -1):
            v = r[j] * Y[j]
            for k in range(7, j, -1):
                v = v - m[k, j] * V[k]
            V[j] = v
        for g in range(p + 1, 16):
            old = groups[g]
            base = jnp.where(indiag, 0.0, old)
            terms = [jnp.broadcast_to(old[:, lo + j : lo + j + 1], (8, H)) * V[j] for j in range(8)]
            t = ((terms[0] + terms[1]) + (terms[2] + terms[3])) + ((terms[4] + terms[5]) + (terms[6] + terms[7]))
            groups[g] = base - t
    return out


def inverse_block(D, Wref, T, R):
    U = factor_inverse([D[8 * g : 8 * g + 8, :] for g in range(16)], T, R)
    lane = lax.broadcasted_iota(jnp.int32, (8, H), 1)
    sub = lax.broadcasted_iota(jnp.int32, (8, H), 0)
    for g in range(16):
        Wref[8 * g : 8 * g + 8, :] = jnp.where(lane <= sub + 8 * g, U[g], 0.0)


def folded_tile(a_ref, nb, i, k):
    upper = i >= nb // 2
    a = jnp.where(upper, nb - 1 - i, i)
    j = jnp.where(upper, k, nb - i + k)
    return a_ref[pl.ds(pl.multiple_of(a * B, B), B), pl.ds(pl.multiple_of(j * B, B), B)]


def kernel(n, a_ref, e_ref, x_ref, lhi, llo, c, ec, whi, wlo, D, W, T, R, z):
    nb = n // B
    diag = lax.broadcasted_iota(jnp.int32, (H, H), 0) == lax.broadcasted_iota(jnp.int32, (H, H), 1)
    damp = jnp.where(diag, jnp.float32(0.2), jnp.float32(0.0))

    def inner(k, _):
        rows_k = pl.ds(pl.multiple_of(k * B, B), B)
        for kk in range(nb):
            @pl.when(k == kk)
            def _():
                cols = slice(kk * B, kk * B + B)
                w = kk * B
                if kk == 0:
                    ec[...] = e_ref[:, cols]

                    @pl.loop(0, nb)
                    def _(i):
                        c[pl.ds(pl.multiple_of(i * B, B), B), :] = folded_tile(a_ref, nb, i, 0)
                else:
                    bh, bl = lhi[w : w + B, :w], llo[w : w + B, :w]
                    eh, el = lhi[n : n + 16, :w], llo[n : n + 16, :w]
                    ec[...] = e_ref[:, cols] - dot3(eh, el, bh, bl, NT)

                    @pl.loop(kk, nb)
                    def _(i):
                        ri = pl.ds(pl.multiple_of(i * B, B), B)
                        c[ri, :] = folded_tile(a_ref, nb, i, kk) - dot3(lhi[ri, :w], llo[ri, :w], bh, bl, NT)

        d0 = pl.multiple_of(k * B, B)
        D[0] = c[pl.ds(d0, H), 0:H] + damp
        inverse_block_ref(D, W, T, R, 0)
        c21 = c[pl.ds(d0 + H, H), 0:H]
        W1 = W[0]
        l21 = mm(c21, W1, NT)
        D[1] = c[pl.ds(d0 + H, H), H:B] + damp - mm(l21, l21, NT)
        inverse_block_ref(D, W, T, R, 1)
        W2 = W[1]
        w21 = -mm(W2, mm(l21, W1, NN), NN)
        zero = jnp.zeros((H, H), jnp.float32)
        full = jnp.concatenate(
            [jnp.concatenate([W1, zero], 1), jnp.concatenate([w21, W2], 1)], 0
        )
        wh, wl = split(full)
        whi[k], wlo[k] = wh, wl
        for kk in range(nb):
            @pl.when(k == kk)
            def _():
                cols = slice(kk * B, kk * B + B)

                @pl.loop(kk + 1, nb)
                def _(i):
                    ri = pl.ds(pl.multiple_of(i * B, B), B)
                    ch, cl = split(c[ri, :])
                    lhi[ri, cols], llo[ri, cols] = split(dot3(ch, cl, wh, wl, NT))

                eh, el = split(ec[...])
                y = dot3(eh, el, wh, wl, NT)
                lhi[n : n + 16, cols], llo[n : n + 16, cols] = split(y)
                z[:, cols] = y
        return 0

    lax.fori_loop(0, nb, inner, 0)
    for kk in range(nb - 1, -1, -1):
        cols = slice(kk * B, kk * B + B)
        zh, zl = split(z[:, cols])
        x = dot3(zh, zl, whi[kk], wlo[kk], NN)
        x_ref[:, cols] = x
        if kk > 0:
            xh, xl = split(x)
            z[:, : kk * B] -= dot3(xh, xl, lhi[cols, : kk * B], llo[cols, : kk * B], NN)


def inverse_block_ref(D, W, T, R, h):
    inverse_block(D[h], W.at[h], T, R)


def solve(a, eps):
    n = eps.shape[0]
    e = jnp.zeros((16, n), jnp.float32).at[0].set(eps)
    nb = n // B
    vm = pl.BlockSpec(memory_space=pltpu.VMEM)
    x = pl.pallas_call(
        functools.partial(kernel, n),
        out_shape=jax.ShapeDtypeStruct((16, n), jnp.float32),
        in_specs=[vm, vm],
        out_specs=vm,
        scratch_shapes=[
            pltpu.VMEM((n + 16, n), jnp.bfloat16),
            pltpu.VMEM((n + 16, n), jnp.bfloat16),
            pltpu.VMEM((n, B), jnp.float32),
            pltpu.VMEM((16, B), jnp.float32),
            pltpu.VMEM((nb, B, B), jnp.bfloat16),
            pltpu.VMEM((nb, B, B), jnp.bfloat16),
            pltpu.VMEM((2, H, H), jnp.float32),
            pltpu.VMEM((2, H, H), jnp.float32),
            pltpu.VMEM((64, H), jnp.float32),
            pltpu.VMEM((8, H), jnp.float32),
            pltpu.VMEM((16, n), jnp.float32),
        ],
        compiler_params=pltpu.CompilerParams(vmem_limit_bytes=60 * 2**20),
    )(a, e)
    return x


MESH = pl.DeviceIdType.MESH
PORTIONS = 6
STEPS = 6


def place():
    smp, par = lax.axis_index("smp"), lax.axis_index("par")
    y, z_lo = lax.div(smp, 2), lax.rem(smp, 2)
    x, z_hi, core = lax.div(par, 4), lax.rem(lax.div(par, 2), 2), lax.rem(par, 2)
    return (x, y, z_hi * 2 + z_lo), core


def device(pos, core):
    x, y, z = pos
    return (y * 2 + lax.rem(z, 2), x * 4 + lax.div(z, 2) * 2 + core)


def plan(pos, core, q):
    out = []
    for stage in range(3):
        axis = (q // 2 + stage) % 3
        i = pos[axis]
        low, high = lax.rem(i, 2), lax.div(i, 2)
        near, far = i + 1 - 2 * low, 3 - i
        if q % 2 == 0:
            order = [(near, lax.rem(low + high, 2)), (far, high)]
        else:
            order = [(far, high), (near, low)]
        for other, bit in order:
            there = list(pos)
            there[axis] = other
            out.append((device(there, core), bit))
    return out


def remote(src, dst, send, recv, who):
    return pltpu.make_async_remote_copy(
        src_ref=src, dst_ref=dst, send_sem=send, recv_sem=recv, device_id=who, device_id_type=MESH
    )


def eight(x):
    return pl.multiple_of(x, 8)


def gram_kernel(total, x_ref, en_ref, O, xa, ebuf, F, recv, xp,
                share_sem, rs_send, rs_recv, ag_send, ag_recv, co_send, co_recv, e_send, e_recv):
    pos, core = place()
    smp, par = lax.axis_index("smp"), lax.axis_index("par")
    n, kp = x_ref.shape
    nb = n // B
    half = F.shape[0]
    width = F.shape[1] // PORTIONS
    plans = [plan(pos, core, q) for q in range(PORTIONS)]
    partner = device(pos, 1 - core)
    others = [(lax.rem(smp + d, 8), par) for d in range(1, 8)]
    peers = [partner] + [plans[2 * a][s][0] for a in range(3) for s in range(2)] + others
    barrier = pltpu.get_barrier_semaphore()
    for who in peers:
        pl.semaphore_signal(barrier, inc=1, device_id=who, device_id_type=MESH)

    scale = 1.0 / np.sqrt(np.float32(total))

    def add(i, acc):
        r = pl.ds(pl.multiple_of(i * 64, 64), 64)
        return acc + jnp.sum(x_ref[r, :].astype(jnp.float32).reshape(8, 8, kp), axis=0)

    acc = lax.fori_loop(0, n // 64, add, jnp.zeros((8, kp), jnp.float32))
    mean = jnp.sum(acc, axis=0, keepdims=True) / total

    @pl.loop(0, n // 64)
    def _(i):
        r = pl.ds(pl.multiple_of(i * 64, 64), 64)
        xa[r, :] = ((x_ref[r, :].astype(jnp.float32) - mean) * scale).astype(jnp.bfloat16)

    ebuf[pl.ds(smp, 1)] = en_ref[...][None]
    pl.semaphore_wait(barrier, len(peers))
    share = remote(xa, xp, share_sem.at[0], share_sem.at[1], partner)
    share.start()
    spread = [remote(en_ref, ebuf.at[smp], e_send.at[d], e_recv.at[d], others[d]) for d in range(7)]
    for copy in spread:
        copy.start()

    def tiles(src, first):
        @pl.loop(0, 2 * (nb + 1))
        def _(t):
            a_local = lax.div(t, nb + 1)
            j = lax.rem(t, nb + 1)
            a = core * (nb // 4) + a_local
            tall = j < nb - a
            r = jnp.where(tall, nb - 1 - a, a)
            cb = jnp.where(tall, j, j - (nb - a))
            rows = src[pl.ds(pl.multiple_of(r * B, B), B), :]
            cols = src[pl.ds(pl.multiple_of(cb * B, B), B), :]
            got = lax.dot_general(rows, cols, (NT, ((), ())), preferred_element_type=jnp.float32)
            at = (pl.ds(pl.multiple_of(a_local * B, B), B), pl.ds(pl.multiple_of(j * B, B), B))
            F[at] = got if first else F[at] + got

    tiles(xa, True)
    share.wait_recv()
    tiles(xp, False)

    def cols(q):
        return slice(q * width, q * width + width)

    offs = [half - (half >> t) for t in range(STEPS)]
    size = [half >> (t + 1) for t in range(STEPS)]
    base = [[jnp.int32(0)] for q in range(PORTIONS)]

    def halving(t, q):
        who, bit = plans[q][t]
        src = F.at[pl.ds(eight(base[q][t] + (1 - bit) * size[t]), size[t]), cols(q)]
        return remote(src, recv.at[pl.ds(offs[t], size[t]), cols(q)], rs_send.at[t, q], rs_recv.at[t, q], who)

    def accumulate(t, q, start, rows):
        at = (pl.ds(eight(base[q][t + 1] + start), rows), cols(q))
        F[at] += recv[pl.ds(eight(offs[t] + start), rows), cols(q)]

    copies = {}
    for q in range(PORTIONS):
        copies[0, q] = halving(0, q)
        copies[0, q].start()
    for t in range(STEPS):
        for q in range(PORTIONS):
            copies[t, q].wait_recv()
            base[q].append(base[q][t] + plans[q][t][1] * size[t])
            if t + 1 < STEPS:
                bit, s = plans[q][t + 1][1], size[t + 1]
                accumulate(t, q, (1 - bit) * s, s)
                copies[t + 1, q] = halving(t + 1, q)
                copies[t + 1, q].start()
                accumulate(t, q, bit * s, s)
            else:
                accumulate(t, q, 0, size[t])

    def region(row, rows, q):
        return O.at[pl.ds(eight(core * half + row), rows), cols(q)]

    def doubling(t, q):
        here = region(base[q][t + 1], size[t], q)
        return remote(here, here, ag_send.at[t, q], ag_recv.at[t, q], plans[q][t][0])

    def across(t, q, row, rows):
        here = region(row, rows, q)
        return remote(here, here, co_send.at[t, q], co_recv.at[t, q], partner)

    back, forth = {}, []
    for q in range(PORTIONS):
        row, rows = base[q][STEPS], size[STEPS - 1]
        O[pl.ds(eight(core * half + row), rows), cols(q)] = F[pl.ds(eight(row), rows), cols(q)]
        back[STEPS - 1, q] = doubling(STEPS - 1, q)
        back[STEPS - 1, q].start()
        forth.append(across(STEPS, q, row, rows))
        forth[-1].start()
    for t in range(STEPS - 1, -1, -1):
        for q in range(PORTIONS):
            back[t, q].wait_recv()
            if t > 0:
                back[t - 1, q] = doubling(t - 1, q)
                back[t - 1, q].start()
            forth.append(across(t, q, base[q][t] + (1 - plans[q][t][1]) * size[t], size[t]))
            forth[-1].start()
    share.wait_send()
    for copy in spread:
        copy.wait()
    for copy in [*copies.values(), *back.values()]:
        copy.wait_send()
    for copy in forth:
        copy.wait()


def damped_gram(mine, energy, total):
    n, kp = mine.shape
    nb = n // B
    wide = (nb + 1) * B
    vm = pl.BlockSpec(memory_space=pltpu.VMEM)
    dma = pltpu.SemaphoreType.DMA
    grid = (STEPS, PORTIONS)
    return pl.pallas_call(
        functools.partial(gram_kernel, total),
        out_shape=[
            jax.ShapeDtypeStruct((n // 2, wide), jnp.float32),
            jax.ShapeDtypeStruct((n, kp), jnp.bfloat16),
            jax.ShapeDtypeStruct((8, 8, 128), jnp.float32),
        ],
        in_specs=[vm, vm],
        out_specs=[vm, vm, vm],
        scratch_shapes=[
            pltpu.VMEM((n // 4, wide), jnp.float32),
            pltpu.VMEM((n // 4, wide), jnp.float32),
            pltpu.VMEM((n, kp), jnp.bfloat16),
            dma((2,)), dma(grid), dma(grid), dma(grid), dma(grid),
            dma((STEPS + 1, PORTIONS)), dma((STEPS + 1, PORTIONS)), dma((7,)), dma((7,)),
        ],
        compiler_params=pltpu.CompilerParams(
            vmem_limit_bytes=48 * 2**20, collective_id=1, has_side_effects=True
        ),
    )(mine, energy)


def update_kernel(x_ref, xc_ref, u_ref, send, recv):
    smp, par = lax.axis_index("smp"), lax.axis_index("par")
    others = [(lax.rem(smp + d, 8), par) for d in range(1, 8)]
    barrier = pltpu.get_barrier_semaphore()
    for who in others:
        pl.semaphore_signal(barrier, inc=1, device_id=who, device_id_type=MESH)
    hi, lo = split(x_ref[...])
    d = lambda a: lax.dot_general(a, xc_ref[...], (NN, ((), ())), preferred_element_type=jnp.float32)
    term = (d(hi) + d(lo))[0:8]
    u_ref[pl.ds(smp, 1)] = term[None]
    pl.semaphore_wait(barrier, len(others))
    here = u_ref.at[smp]
    copies = [remote(here, here, send.at[i], recv.at[i], others[i]) for i in range(7)]
    for copy in copies:
        copy.start()
    for copy in copies:
        copy.wait()


def project(x, xc):
    vm = pl.BlockSpec(memory_space=pltpu.VMEM)
    u = pl.pallas_call(
        update_kernel,
        out_shape=jax.ShapeDtypeStruct((8, 8, xc.shape[1]), jnp.float32),
        in_specs=[vm, vm],
        out_specs=vm,
        scratch_shapes=[pltpu.SemaphoreType.DMA((7,)), pltpu.SemaphoreType.DMA((7,))],
        compiler_params=pltpu.CompilerParams(
            vmem_limit_bytes=32 * 2**20, collective_id=2, has_side_effects=True
        ),
    )(x, xc)
    return u[:, 0, :].reshape(-1)


SIDE = 10


def local_energy(spins):
    sigma = (2 * spins - 1).astype(jnp.float32).reshape(-1, SIDE, SIDE)
    right = jnp.roll(sigma, 1, axis=2)
    below = jnp.roll(sigma, 1, axis=1)
    diag_one = jnp.roll(below, 1, axis=2)
    diag_two = jnp.roll(below, -1, axis=2)
    nearest = jnp.sum(sigma * right + sigma * below, axis=(1, 2))
    second = jnp.sum(sigma * diag_one + sigma * diag_two, axis=(1, 2))
    return 0.25 * nearest + 0.125 * second


def body(log_derivs, spins, hop_energy):
    rows = log_derivs.shape[0]
    total = rows * 8
    scale = 1.0 / jnp.sqrt(jnp.float32(total))
    energy = local_energy(spins) + hop_energy
    energy = jnp.pad(energy.reshape(rows // 128, 128), ((0, 8 - rows // 128), (0, 0)))
    mine = lax.all_to_all(log_derivs, "smp", split_axis=1, concat_axis=0, tiled=True)
    gram, centered, energies = damped_gram(mine, energy, total)
    all_energy = energies[:, : rows // 128].reshape(-1)
    eps = (all_energy - jnp.mean(all_energy)) * scale
    coeffs = solve(gram, eps)
    update = project(coeffs, centered)
    start = lax.axis_index("smp") * rows
    return update, lax.dynamic_slice_in_dim(coeffs[0], start, rows, 0)


def solution(mesh):
    placed = (P("smp", "par"), P("smp", None), P("smp"))
    return jax.shard_map(
        body, mesh=mesh, in_specs=placed, out_specs=(P("par"), P("smp")), check_vma=False
    )
```

```python
import functools
import jax, jax.numpy as jnp
import numpy as np
from jax import lax
from jax.experimental import pallas as pl
from jax.experimental.pallas import tpu as pltpu
from jax.sharding import PartitionSpec as P

B = 256
H = 128
NT = ((1,), (1,))
NN = ((1,), (0,))


def split(x):
    hi = x.astype(jnp.bfloat16)
    return hi, (x - hi.astype(jnp.float32)).astype(jnp.bfloat16)


def dot3(ah, al, bh, bl, dims):
    d = lambda a, b: lax.dot_general(a, b, (dims, ((), ())), preferred_element_type=jnp.float32)
    return d(ah, bh) + (d(ah, bl) + d(al, bh))


def splat(x):
    return jnp.broadcast_to(x, (8, H))


def factor_inverse(groups, T, R, A2, beside):
    lane = lax.broadcasted_iota(jnp.int32, (8, H), 1)
    sub = lax.broadcasted_iota(jnp.int32, (8, H), 0)
    out = []
    corner = [splat(groups[0][:, j : j + 1]) for j in range(8)]
    for p in range(16):
        if beside is not None:
            beside(p)
        lo, slot = 8 * p, p % 2
        pivots, at = groups[p], 64 * slot
        for j in range(8):
            T[at + 8 * j : at + 8 * j + 8, :] = corner[j]
        inside = (lane >= lo) & (lane < lo + 8)
        R[8 * slot : 8 * slot + 8, :] = jnp.where(inside, (lane - lo == sub).astype(jnp.float32), pivots)
        e = {}
        for j in range(8):
            for i in range(j, 8):
                e[i, j] = splat(T[at + 8 * j + i : at + 8 * j + i + 1, :])
        y = [splat(R[8 * slot + i : 8 * slot + i + 1, :]) for i in range(8)]
        last = p == 15
        if not last:
            near = groups[p + 1]
            a = [splat(near[:, lo + j : lo + j + 1]) for j in range(8)]
            corner = [splat(near[:, lo + 8 + j : lo + 9 + j]) for j in range(8)]
            near = jnp.where(inside, 0.0, near)
        m, r, u = {}, [], None
        for k in range(8):
            rk = pl.reciprocal(e[k, k], approx=True)
            r.append(rk)
            for i in range(k + 1, 8):
                m[i, k] = e[i, k] * rk
            for i in range(k + 1, 8):
                for q in range(k + 1, i + 1):
                    if i == q == k + 1:
                        e[i, q] = e[i, q] - (e[i, k] * e[i, k]) * rk
                    else:
                        e[i, q] = e[i, q] - m[i, k] * e[q, k]
            for i in range(k + 1, 8):
                y[i] = y[i] - m[i, k] * y[k]
            row = y[k] * lax.rsqrt(e[k, k])
            u = row if k == 0 else jnp.where(sub == k, row, u)
            if not last:
                for i in range(k + 1, 8):
                    a[i] = a[i] - m[i, k] * a[k]
                scaled = a[k] * rk
                A2[at + 8 * k : at + 8 * k + 8, :] = scaled
                near = near - scaled * y[k]
                for j in range(8):
                    corner[j] = corner[j] - a[k] * splat(A2[at + 8 * k + j : at + 8 * k + j + 1, :])
        out.append(u)
        if last:
            break
        groups[p + 1] = near
        v = [None] * 8
        for j in range(7, -1, -1):
            t = r[j] * y[j]
            for k in range(7, j, -1):
                t = t - m[k, j] * v[k]
            v[j] = t
        for g in range(p + 2, 16):
            old = groups[g]
            t = [splat(old[:, lo + j : lo + j + 1]) * v[j] for j in range(8)]
            t = ((t[0] + t[1]) + (t[2] + t[3])) + ((t[4] + t[5]) + (t[6] + t[7]))
            groups[g] = jnp.where(inside, 0.0, old) - t
    return [jnp.where(lane <= sub + 8 * g, out[g], 0.0) for g in range(16)]


def tile(nb, i, k):
    upper = i >= nb // 2
    a = jnp.where(upper, nb - 1 - i, i)
    j = jnp.where(upper, k, nb - i + k)
    return pl.ds(pl.multiple_of(a * B, B), B), pl.ds(pl.multiple_of(j * B, B), B)


def block(i):
    return pl.ds(pl.multiple_of(i * B, B), B)


SLOTS = 8


def kernel(n, g_ref, e_ref, x_ref, G, lhi, llo, ec, whi, wlo, D, W, T, R, A2, z, sem):
    nb = n // B
    load = pltpu.make_async_copy(g_ref, G.at[0 : n // 2, :], sem)
    load.start()
    ec[...] = e_ref[...]
    diag = lax.broadcasted_iota(jnp.int32, (H, H), 0) == lax.broadcasted_iota(jnp.int32, (H, H), 1)
    damp = jnp.where(diag, jnp.float32(0.2), jnp.float32(0.0))
    load.wait()

    def triangle(k, i):
        ch, cl = split(G[tile(nb, i, k)])
        th, tl = split(dot3(ch, cl, whi[k], wlo[k], NT))
        lhi[block(i), block(k)], llo[block(i), block(k)] = th, tl
        yh, yl = split(z[:, block(k)])
        ec[:, block(i)] -= dot3(yh, yl, th, tl, NT)
        return th, tl

    def factor(k, h, slots):
        def beside(p):
            if p % (16 // SLOTS) != 0:
                return
            s = h * SLOTS + p // (16 // SLOTS)
            live = s < (k + 1) * (nb - 1 - k)
            i = jnp.minimum(k + 1 + lax.div(s, k + 1), nb - 1)
            u = lax.rem(s, k + 1)
            own = u == k
            column = jnp.where(own, k, jnp.minimum(k + 1, nb - 1))
            j = jnp.where(own, k - 1, u)
            rows, cols = tile(nb, i, column)
            rows = pl.ds(pl.multiple_of(jnp.where(live, rows.start, n // 2), B), B)
            G[rows, cols] -= dot3(
                lhi[block(i), block(j)], llo[block(i), block(j)],
                lhi[block(column), block(j)], llo[block(column), block(j)], NT)

        got = factor_inverse([D[8 * g : 8 * g + 8, :] for g in range(16)], T, R, A2, beside if slots else None)
        for g in range(16):
            W[h, 8 * g : 8 * g + 8, :] = got[g]

    def chain(k, h):
        some = (k > 0) & (k < nb - 1)

        @pl.when(some)
        def _():
            factor(k, h, True)

        @pl.when(jnp.logical_not(some))
        def _():
            factor(k, h, False)

    def panel(k, _):
        rows, cols = tile(nb, k, k)
        r0, c0 = rows.start, cols.start

        @pl.when(k > 0)
        def _():
            th, tl = triangle(k - 1, k)
            G[rows, cols] -= dot3(th, tl, th, tl, NT)

            @pl.loop(k + 1, nb)
            def _(i):
                triangle(k - 1, i)

        top, low = pl.ds(r0, H), pl.ds(pl.multiple_of(r0 + H, H), H)
        left, right = pl.ds(c0, H), pl.ds(pl.multiple_of(c0 + H, H), H)
        D[...] = G[top, left] + damp
        chain(k, 0)
        w1h, w1l = split(W[0])
        ah, al = split(G[low, left])
        lh, ll = split(dot3(ah, al, w1h, w1l, NT))
        D[...] = G[low, right] + damp - dot3(lh, ll, lh, ll, NT)
        th, tl = split(dot3(lh, ll, w1h, w1l, NN))
        whi[k, 0:H, 0:H], wlo[k, 0:H, 0:H] = w1h, w1l
        whi[k, 0:H, H:B] = jnp.zeros((H, H), jnp.bfloat16)
        wlo[k, 0:H, H:B] = jnp.zeros((H, H), jnp.bfloat16)
        chain(k, 1)
        w2h, w2l = split(W[1])
        whi[k, H:B, H:B], wlo[k, H:B, H:B] = w2h, w2l
        whi[k, H:B, 0:H], wlo[k, H:B, 0:H] = split(-dot3(w2h, w2l, th, tl, NN))
        eh, el = split(ec[:, block(k)])
        z[:, block(k)] = dot3(eh, el, whi[k], wlo[k], NT)
        return 0

    lax.fori_loop(0, nb, panel, 0)
    for kk in range(nb - 1, -1, -1):
        cols = slice(kk * B, kk * B + B)
        zh, zl = split(z[:, cols])
        x = dot3(zh, zl, whi[kk], wlo[kk], NN)
        x_ref[:, cols] = x
        if kk > 0:
            xh, xl = split(x)
            z[:, : kk * B] -= dot3(xh, xl, lhi[cols, : kk * B], llo[cols, : kk * B], NN)


def solve(a, eps):
    n = eps.shape[0]
    e = jnp.zeros((16, n), jnp.float32).at[0].set(eps)
    nb = n // B
    vm = pl.BlockSpec(memory_space=pltpu.VMEM)
    return pl.pallas_call(
        functools.partial(kernel, n),
        out_shape=jax.ShapeDtypeStruct((16, n), jnp.float32),
        in_specs=[pl.BlockSpec(memory_space=pl.ANY), vm],
        out_specs=vm,
        scratch_shapes=[
            pltpu.VMEM((n // 2 + B, (nb + 1) * B), jnp.float32),
            pltpu.VMEM((n, n), jnp.bfloat16),
            pltpu.VMEM((n, n), jnp.bfloat16),
            pltpu.VMEM((16, n), jnp.float32),
            pltpu.VMEM((nb, B, B), jnp.bfloat16),
            pltpu.VMEM((nb, B, B), jnp.bfloat16),
            pltpu.VMEM((H, H), jnp.float32),
            pltpu.VMEM((2, H, H), jnp.float32),
            pltpu.VMEM((128, H), jnp.float32),
            pltpu.VMEM((16, H), jnp.float32),
            pltpu.VMEM((128, H), jnp.float32),
            pltpu.VMEM((16, n), jnp.float32),
            pltpu.SemaphoreType.DMA,
        ],
        compiler_params=pltpu.CompilerParams(vmem_limit_bytes=56 * 2**20),
    )(a, e)


MESH = pl.DeviceIdType.MESH
PORTIONS = 6
STEPS = 6


def place():
    smp, par = lax.axis_index("smp"), lax.axis_index("par")
    y, z_lo = lax.div(smp, 2), lax.rem(smp, 2)
    x, z_hi, core = lax.div(par, 4), lax.rem(lax.div(par, 2), 2), lax.rem(par, 2)
    return (x, y, z_hi * 2 + z_lo), core


def device(pos, core):
    x, y, z = pos
    return (y * 2 + lax.rem(z, 2), x * 4 + lax.div(z, 2) * 2 + core)


def plan(pos, core, q):
    out = []
    for stage in range(3):
        axis = (q // 2 + stage) % 3
        i = pos[axis]
        low, high = lax.rem(i, 2), lax.div(i, 2)
        near, far = i + 1 - 2 * low, 3 - i
        if q % 2 == 0:
            order = [(near, lax.rem(low + high, 2)), (far, high)]
        else:
            order = [(far, high), (near, low)]
        for other, bit in order:
            there = list(pos)
            there[axis] = other
            out.append((device(there, core), bit))
    return out


def remote(src, dst, send, recv, who):
    return pltpu.make_async_remote_copy(
        src_ref=src, dst_ref=dst, send_sem=send, recv_sem=recv, device_id=who, device_id_type=MESH
    )


def eight(x):
    return pl.multiple_of(x, 8)


def gram_kernel(total, x_ref, en_ref, O, xa, ebuf, F, recv, xp,
                share_sem, rs_send, rs_recv, ag_send, ag_recv, co_send, co_recv, e_send, e_recv):
    pos, core = place()
    smp, par = lax.axis_index("smp"), lax.axis_index("par")
    n, kp = x_ref.shape
    nb = n // B
    half = F.shape[0]
    width = F.shape[1] // PORTIONS
    plans = [plan(pos, core, q) for q in range(PORTIONS)]
    partner = device(pos, 1 - core)
    others = [(lax.rem(smp + d, 8), par) for d in range(1, 8)]
    peers = [partner] + [plans[2 * a][s][0] for a in range(3) for s in range(2)] + others
    barrier = pltpu.get_barrier_semaphore()
    for who in peers:
        pl.semaphore_signal(barrier, inc=1, device_id=who, device_id_type=MESH)

    scale = 1.0 / np.sqrt(np.float32(total))

    def add(i, acc):
        r = pl.ds(pl.multiple_of(i * 64, 64), 64)
        return acc + jnp.sum(x_ref[r, :].astype(jnp.float32).reshape(8, 8, kp), axis=0)

    acc = lax.fori_loop(0, n // 64, add, jnp.zeros((8, kp), jnp.float32))
    mean = jnp.sum(acc, axis=0, keepdims=True) / total

    @pl.loop(0, n // 64)
    def _(i):
        r = pl.ds(pl.multiple_of(i * 64, 64), 64)
        xa[r, :] = ((x_ref[r, :].astype(jnp.float32) - mean) * scale).astype(jnp.bfloat16)

    ebuf[pl.ds(smp, 1)] = en_ref[...][None]
    pl.semaphore_wait(barrier, len(peers))
    share = remote(xa, xp, share_sem.at[0], share_sem.at[1], partner)
    share.start()
    spread = [remote(en_ref, ebuf.at[smp], e_send.at[d], e_recv.at[d], others[d]) for d in range(7)]
    for copy in spread:
        copy.start()

    def tiles(src, first):
        @pl.loop(0, 2 * (nb + 1))
        def _(t):
            a_local = lax.div(t, nb + 1)
            j = lax.rem(t, nb + 1)
            a = core * (nb // 4) + a_local
            tall = j < nb - a
            r = jnp.where(tall, nb - 1 - a, a)
            cb = jnp.where(tall, j, j - (nb - a))
            rows = src[pl.ds(pl.multiple_of(r * B, B), B), :]
            cols = src[pl.ds(pl.multiple_of(cb * B, B), B), :]
            got = lax.dot_general(rows, cols, (NT, ((), ())), preferred_element_type=jnp.float32)
            at = (pl.ds(pl.multiple_of(a_local * B, B), B), pl.ds(pl.multiple_of(j * B, B), B))
            F[at] = got if first else F[at] + got

    tiles(xa, True)
    share.wait_recv()
    tiles(xp, False)

    def cols(q):
        return slice(q * width, q * width + width)

    offs = [half - (half >> t) for t in range(STEPS)]
    size = [half >> (t + 1) for t in range(STEPS)]
    base = [[jnp.int32(0)] for q in range(PORTIONS)]

    def halving(t, q):
        who, bit = plans[q][t]
        src = F.at[pl.ds(eight(base[q][t] + (1 - bit) * size[t]), size[t]), cols(q)]
        return remote(src, recv.at[pl.ds(offs[t], size[t]), cols(q)], rs_send.at[t, q], rs_recv.at[t, q], who)

    def accumulate(t, q, start, rows):
        at = (pl.ds(eight(base[q][t + 1] + start), rows), cols(q))
        F[at] += recv[pl.ds(eight(offs[t] + start), rows), cols(q)]

    copies = {}
    for q in range(PORTIONS):
        copies[0, q] = halving(0, q)
        copies[0, q].start()
    for t in range(STEPS):
        for q in range(PORTIONS):
            copies[t, q].wait_recv()
            base[q].append(base[q][t] + plans[q][t][1] * size[t])
            if t + 1 < STEPS:
                bit, s = plans[q][t + 1][1], size[t + 1]
                accumulate(t, q, (1 - bit) * s, s)
                copies[t + 1, q] = halving(t + 1, q)
                copies[t + 1, q].start()
                accumulate(t, q, bit * s, s)
            else:
                accumulate(t, q, 0, size[t])

    def region(row, rows, q):
        return O.at[pl.ds(eight(core * half + row), rows), cols(q)]

    def doubling(t, q):
        here = region(base[q][t + 1], size[t], q)
        return remote(here, here, ag_send.at[t, q], ag_recv.at[t, q], plans[q][t][0])

    def across(t, q, row, rows):
        here = region(row, rows, q)
        return remote(here, here, co_send.at[t, q], co_recv.at[t, q], partner)

    back, forth = {}, []
    for q in range(PORTIONS):
        row, rows = base[q][STEPS], size[STEPS - 1]
        O[pl.ds(eight(core * half + row), rows), cols(q)] = F[pl.ds(eight(row), rows), cols(q)]
        back[STEPS - 1, q] = doubling(STEPS - 1, q)
        back[STEPS - 1, q].start()
        forth.append(across(STEPS, q, row, rows))
        forth[-1].start()
    for t in range(STEPS - 1, -1, -1):
        for q in range(PORTIONS):
            back[t, q].wait_recv()
            if t > 0:
                back[t - 1, q] = doubling(t - 1, q)
                back[t - 1, q].start()
            forth.append(across(t, q, base[q][t] + (1 - plans[q][t][1]) * size[t], size[t]))
            forth[-1].start()
    share.wait_send()
    for copy in spread:
        copy.wait()
    for copy in [*copies.values(), *back.values()]:
        copy.wait_send()
    for copy in forth:
        copy.wait()


def damped_gram(mine, energy, total):
    n, kp = mine.shape
    nb = n // B
    wide = (nb + 1) * B
    vm = pl.BlockSpec(memory_space=pltpu.VMEM)
    dma = pltpu.SemaphoreType.DMA
    grid = (STEPS, PORTIONS)
    return pl.pallas_call(
        functools.partial(gram_kernel, total),
        out_shape=[
            jax.ShapeDtypeStruct((n // 2, wide), jnp.float32),
            jax.ShapeDtypeStruct((n, kp), jnp.bfloat16),
            jax.ShapeDtypeStruct((8, 8, 128), jnp.float32),
        ],
        in_specs=[vm, vm],
        out_specs=[vm, vm, vm],
        scratch_shapes=[
            pltpu.VMEM((n // 4, wide), jnp.float32),
            pltpu.VMEM((n // 4, wide), jnp.float32),
            pltpu.VMEM((n, kp), jnp.bfloat16),
            dma((2,)), dma(grid), dma(grid), dma(grid), dma(grid),
            dma((STEPS + 1, PORTIONS)), dma((STEPS + 1, PORTIONS)), dma((7,)), dma((7,)),
        ],
        compiler_params=pltpu.CompilerParams(
            vmem_limit_bytes=48 * 2**20, collective_id=1, has_side_effects=True
        ),
    )(mine, energy)


def update_kernel(x_ref, xc_ref, u_ref, send, recv):
    smp, par = lax.axis_index("smp"), lax.axis_index("par")
    others = [(lax.rem(smp + d, 8), par) for d in range(1, 8)]
    barrier = pltpu.get_barrier_semaphore()
    for who in others:
        pl.semaphore_signal(barrier, inc=1, device_id=who, device_id_type=MESH)
    hi, lo = split(x_ref[...])
    d = lambda a: lax.dot_general(a, xc_ref[...], (NN, ((), ())), preferred_element_type=jnp.float32)
    term = (d(hi) + d(lo))[0:8]
    u_ref[pl.ds(smp, 1)] = term[None]
    pl.semaphore_wait(barrier, len(others))
    here = u_ref.at[smp]
    copies = [remote(here, here, send.at[i], recv.at[i], others[i]) for i in range(7)]
    for copy in copies:
        copy.start()
    for copy in copies:
        copy.wait()


def project(x, xc):
    vm = pl.BlockSpec(memory_space=pltpu.VMEM)
    u = pl.pallas_call(
        update_kernel,
        out_shape=jax.ShapeDtypeStruct((8, 8, xc.shape[1]), jnp.float32),
        in_specs=[vm, vm],
        out_specs=vm,
        scratch_shapes=[pltpu.SemaphoreType.DMA((7,)), pltpu.SemaphoreType.DMA((7,))],
        compiler_params=pltpu.CompilerParams(
            vmem_limit_bytes=32 * 2**20, collective_id=2, has_side_effects=True
        ),
    )(x, xc)
    return u[:, 0, :].reshape(-1)


SIDE = 10


def local_energy(spins):
    sigma = (2 * spins - 1).astype(jnp.float32).reshape(-1, SIDE, SIDE)
    right = jnp.roll(sigma, 1, axis=2)
    below = jnp.roll(sigma, 1, axis=1)
    diag_one = jnp.roll(below, 1, axis=2)
    diag_two = jnp.roll(below, -1, axis=2)
    nearest = jnp.sum(sigma * right + sigma * below, axis=(1, 2))
    second = jnp.sum(sigma * diag_one + sigma * diag_two, axis=(1, 2))
    return 0.25 * nearest + 0.125 * second


def body(log_derivs, spins, hop_energy):
    rows = log_derivs.shape[0]
    total = rows * 8
    scale = 1.0 / jnp.sqrt(jnp.float32(total))
    energy = local_energy(spins) + hop_energy
    energy = jnp.pad(energy.reshape(rows // 128, 128), ((0, 8 - rows // 128), (0, 0)))
    mine = lax.all_to_all(log_derivs, "smp", split_axis=1, concat_axis=0, tiled=True)
    gram, centered, energies = damped_gram(mine, energy, total)
    all_energy = energies[:, : rows // 128].reshape(-1)
    eps = (all_energy - jnp.mean(all_energy)) * scale
    coeffs = solve(gram, eps)
    update = project(coeffs, centered)
    start = lax.axis_index("smp") * rows
    return update, lax.dynamic_slice_in_dim(coeffs[0], start, rows, 0)


def solution(mesh):
    placed = (P("smp", "par"), P("smp", None), P("smp"))
    return jax.shard_map(
        body, mesh=mesh, in_specs=placed, out_specs=(P("par"), P("smp")), check_vma=False
    )
```

```python
import functools
import jax, jax.numpy as jnp
import numpy as np
from jax import lax
from jax.experimental import pallas as pl
from jax.experimental.pallas import tpu as pltpu
from jax.sharding import PartitionSpec as P

B = 256
H = 128
NT = ((1,), (1,))
NN = ((1,), (0,))


def split(x):
    hi = x.astype(jnp.bfloat16)
    return hi, (x - hi.astype(jnp.float32)).astype(jnp.bfloat16)


def dot3(ah, al, bh, bl, dims):
    d = lambda a, b: lax.dot_general(a, b, (dims, ((), ())), preferred_element_type=jnp.float32)
    return d(ah, bh) + (d(ah, bl) + d(al, bh))


def splat(x):
    return jnp.broadcast_to(x, (8, H))


def factor_inverse(groups, T, R, A2, beside):
    lane = lax.broadcasted_iota(jnp.int32, (8, H), 1)
    sub = lax.broadcasted_iota(jnp.int32, (8, H), 0)
    out = []
    corner = [splat(groups[0][:, j : j + 1]) for j in range(8)]
    for p in range(16):
        if beside is not None:
            beside(p)
        lo, slot = 8 * p, p % 2
        pivots, at = groups[p], 64 * slot
        for j in range(8):
            T[at + 8 * j : at + 8 * j + 8, :] = corner[j]
        inside = (lane >= lo) & (lane < lo + 8)
        R[8 * slot : 8 * slot + 8, :] = jnp.where(inside, (lane - lo == sub).astype(jnp.float32), pivots)
        e = {}
        for j in range(8):
            for i in range(j, 8):
                e[i, j] = splat(T[at + 8 * j + i : at + 8 * j + i + 1, :])
        y = [splat(R[8 * slot + i : 8 * slot + i + 1, :]) for i in range(8)]
        last = p == 15
        if not last:
            near = groups[p + 1]
            a = [splat(near[:, lo + j : lo + j + 1]) for j in range(8)]
            corner = [splat(near[:, lo + 8 + j : lo + 9 + j]) for j in range(8)]
            near = jnp.where(inside, 0.0, near)
        m, r, u = {}, [], None
        for k in range(8):
            rk = pl.reciprocal(e[k, k], approx=True)
            r.append(rk)
            for i in range(k + 1, 8):
                m[i, k] = e[i, k] * rk
            for i in range(k + 1, 8):
                for q in range(k + 1, i + 1):
                    if i == q == k + 1:
                        e[i, q] = e[i, q] - (e[i, k] * e[i, k]) * rk
                    else:
                        e[i, q] = e[i, q] - m[i, k] * e[q, k]
            for i in range(k + 1, 8):
                y[i] = y[i] - m[i, k] * y[k]
            row = y[k] * lax.rsqrt(e[k, k])
            u = row if k == 0 else jnp.where(sub == k, row, u)
            if not last:
                for i in range(k + 1, 8):
                    a[i] = a[i] - m[i, k] * a[k]
                scaled = a[k] * rk
                A2[at + 8 * k : at + 8 * k + 8, :] = scaled
                near = near - scaled * y[k]
                for j in range(8):
                    corner[j] = corner[j] - a[k] * splat(A2[at + 8 * k + j : at + 8 * k + j + 1, :])
        out.append(u)
        if last:
            break
        groups[p + 1] = near
        v = [None] * 8
        for j in range(7, -1, -1):
            t = r[j] * y[j]
            for k in range(7, j, -1):
                t = t - m[k, j] * v[k]
            v[j] = t
        for g in range(p + 2, 16):
            old = groups[g]
            t = [splat(old[:, lo + j : lo + j + 1]) * v[j] for j in range(8)]
            t = ((t[0] + t[1]) + (t[2] + t[3])) + ((t[4] + t[5]) + (t[6] + t[7]))
            groups[g] = jnp.where(inside, 0.0, old) - t
    return [jnp.where(lane <= sub + 8 * g, out[g], 0.0) for g in range(16)]


def tile(nb, i, k):
    upper = i >= nb // 2
    a = jnp.where(upper, nb - 1 - i, i)
    j = jnp.where(upper, k, nb - i + k)
    return pl.ds(pl.multiple_of(a * B, B), B), pl.ds(pl.multiple_of(j * B, B), B)


def block(i):
    return pl.ds(pl.multiple_of(i * B, B), B)


SLOTS = 8


def kernel(n, g_ref, e_ref, x_ref, G, lhi, llo, ec, whi, wlo, D, W, T, R, A2, z, sem):
    nb = n // B
    load = pltpu.make_async_copy(g_ref, G.at[0 : n // 2, :], sem)
    load.start()
    ec[...] = e_ref[...]
    diag = lax.broadcasted_iota(jnp.int32, (H, H), 0) == lax.broadcasted_iota(jnp.int32, (H, H), 1)
    damp = jnp.where(diag, jnp.float32(0.2), jnp.float32(0.0))
    load.wait()

    def triangle(k, i):
        ch, cl = split(G[tile(nb, i, k)])
        th, tl = split(dot3(ch, cl, whi[k], wlo[k], NT))
        lhi[block(i), block(k)], llo[block(i), block(k)] = th, tl
        yh, yl = split(z[:, block(k)])
        ec[:, block(i)] -= dot3(yh, yl, th, tl, NT)
        return th, tl

    def factor(k, h, slots):
        def beside(p):
            if p % (16 // SLOTS) != 0:
                return
            s = h * SLOTS + p // (16 // SLOTS)
            live = s < (k + 1) * (nb - 1 - k)
            i = jnp.minimum(k + 1 + lax.div(s, k + 1), nb - 1)
            u = lax.rem(s, k + 1)
            own = u == k
            column = jnp.where(own, k, jnp.minimum(k + 1, nb - 1))
            j = jnp.where(own, k - 1, u)
            rows, cols = tile(nb, i, column)
            rows = pl.ds(pl.multiple_of(jnp.where(live, rows.start, n // 2), B), B)
            G[rows, cols] -= dot3(
                lhi[block(i), block(j)], llo[block(i), block(j)],
                lhi[block(column), block(j)], llo[block(column), block(j)], NT)

        got = factor_inverse([D[8 * g : 8 * g + 8, :] for g in range(16)], T, R, A2, beside if slots else None)
        for g in range(16):
            W[h, 8 * g : 8 * g + 8, :] = got[g]

    def chain(k, h):
        some = (k > 0) & (k < nb - 1)

        @pl.when(some)
        def _():
            factor(k, h, True)

        @pl.when(jnp.logical_not(some))
        def _():
            factor(k, h, False)

    def panel(k, _):
        rows, cols = tile(nb, k, k)
        r0, c0 = rows.start, cols.start

        @pl.when(k > 0)
        def _():
            th, tl = triangle(k - 1, k)
            G[rows, cols] -= dot3(th, tl, th, tl, NT)

            @pl.loop(k + 1, nb)
            def _(i):
                triangle(k - 1, i)

        top, low = pl.ds(r0, H), pl.ds(pl.multiple_of(r0 + H, H), H)
        left, right = pl.ds(c0, H), pl.ds(pl.multiple_of(c0 + H, H), H)
        D[...] = G[top, left] + damp
        chain(k, 0)
        w1h, w1l = split(W[0])
        ah, al = split(G[low, left])
        lh, ll = split(dot3(ah, al, w1h, w1l, NT))
        D[...] = G[low, right] + damp - dot3(lh, ll, lh, ll, NT)
        th, tl = split(dot3(lh, ll, w1h, w1l, NN))
        whi[k, 0:H, 0:H], wlo[k, 0:H, 0:H] = w1h, w1l
        whi[k, 0:H, H:B] = jnp.zeros((H, H), jnp.bfloat16)
        wlo[k, 0:H, H:B] = jnp.zeros((H, H), jnp.bfloat16)
        chain(k, 1)
        w2h, w2l = split(W[1])
        whi[k, H:B, H:B], wlo[k, H:B, H:B] = w2h, w2l
        whi[k, H:B, 0:H], wlo[k, H:B, 0:H] = split(-dot3(w2h, w2l, th, tl, NN))
        eh, el = split(ec[:, block(k)])
        z[:, block(k)] = dot3(eh, el, whi[k], wlo[k], NT)
        return 0

    lax.fori_loop(0, nb, panel, 0)
    for kk in range(nb - 1, -1, -1):
        cols = slice(kk * B, kk * B + B)
        zh, zl = split(z[:, cols])
        x = dot3(zh, zl, whi[kk], wlo[kk], NN)
        x_ref[:, cols] = x
        if kk > 0:
            xh, xl = split(x)
            z[:, : kk * B] -= dot3(xh, xl, lhi[cols, : kk * B], llo[cols, : kk * B], NN)


def solve(a, eps):
    n = eps.shape[0]
    e = jnp.zeros((16, n), jnp.float32).at[0].set(eps)
    nb = n // B
    vm = pl.BlockSpec(memory_space=pltpu.VMEM)
    return pl.pallas_call(
        functools.partial(kernel, n),
        out_shape=jax.ShapeDtypeStruct((16, n), jnp.float32),
        in_specs=[pl.BlockSpec(memory_space=pl.ANY), vm],
        out_specs=vm,
        scratch_shapes=[
            pltpu.VMEM((n // 2 + B, (nb + 1) * B), jnp.float32),
            pltpu.VMEM((n, n), jnp.bfloat16),
            pltpu.VMEM((n, n), jnp.bfloat16),
            pltpu.VMEM((16, n), jnp.float32),
            pltpu.VMEM((nb, B, B), jnp.bfloat16),
            pltpu.VMEM((nb, B, B), jnp.bfloat16),
            pltpu.VMEM((H, H), jnp.float32),
            pltpu.VMEM((2, H, H), jnp.float32),
            pltpu.VMEM((128, H), jnp.float32),
            pltpu.VMEM((16, H), jnp.float32),
            pltpu.VMEM((128, H), jnp.float32),
            pltpu.VMEM((16, n), jnp.float32),
            pltpu.SemaphoreType.DMA,
        ],
        compiler_params=pltpu.CompilerParams(vmem_limit_bytes=56 * 2**20),
    )(a, e)


MESH = pl.DeviceIdType.MESH
PORTIONS = 6
STEPS = 6
CHUNKS = 2


def place():
    smp, par = lax.axis_index("smp"), lax.axis_index("par")
    y, z_lo = lax.div(smp, 2), lax.rem(smp, 2)
    x, z_hi, core = lax.div(par, 4), lax.rem(lax.div(par, 2), 2), lax.rem(par, 2)
    return (x, y, z_hi * 2 + z_lo), core


def device(pos, core):
    x, y, z = pos
    return (y * 2 + lax.rem(z, 2), x * 4 + lax.div(z, 2) * 2 + core)


def plan(pos, core, q):
    out = []
    for stage in range(3):
        axis = (q // 2 + stage) % 3
        i = pos[axis]
        low, high = lax.rem(i, 2), lax.div(i, 2)
        near, far = i + 1 - 2 * low, 3 - i
        if q % 2 == 0:
            order = [(near, lax.rem(low + high, 2)), (far, high)]
        else:
            order = [(far, high), (near, low)]
        for other, bit in order:
            there = list(pos)
            there[axis] = other
            out.append((device(there, core), bit))
    return out


def remote(src, dst, send, recv, who):
    return pltpu.make_async_remote_copy(
        src_ref=src, dst_ref=dst, send_sem=send, recv_sem=recv, device_id=who, device_id_type=MESH
    )


def eight(x):
    return pl.multiple_of(x, 8)


def gram_kernel(total, x_ref, en_ref, O, xa, ebuf, F, recv, raw, xp, relay,
                share_sem, rs_send, rs_recv, ag_send, ag_recv, co_send, co_recv, e_send, e_recv,
                a_send, a_recv, own_sem):
    pos, core = place()
    smp, par = lax.axis_index("smp"), lax.axis_index("par")
    n, kp = raw.shape
    nr = x_ref.shape[0]
    kc = kp // CHUNKS
    nb = n // B
    half = F.shape[0]
    width = F.shape[1] // PORTIONS
    plans = [plan(pos, core, q) for q in range(PORTIONS)]
    partner = device(pos, 1 - core)
    others = [(lax.rem(smp + d, 8), par) for d in range(1, 8)]
    peers = [partner] + [plans[2 * a][s][0] for a in range(3) for s in range(2)] + others
    barrier = pltpu.get_barrier_semaphore()
    for who in peers:
        pl.semaphore_signal(barrier, inc=1, device_id=who, device_id_type=MESH)

    y, z_lo = lax.div(smp, 2), lax.rem(smp, 2)

    def seat(dy, dz):
        return lax.rem(y + dy + 4, 4) * 2 + (1 - z_lo if dz else z_lo)

    def sent(to, c):
        return pl.ds(pl.multiple_of(to * kp + c * kc, kc), kc)

    def landing(origin, row, rows, c):
        return raw.at[pl.ds(pl.multiple_of(origin * nr + row, rows), rows), c * kc : (c + 1) * kc]

    def straight(c):
        out = []
        for i, (dy, dz) in enumerate([(1, 0), (-1, 0), (1, 1), (-1, 1), (0, 1)]):
            to = seat(dy, dz)
            out.append(remote(x_ref.at[:, sent(to, c)], landing(smp, 0, nr, c), a_send.at[c, i], a_recv.at[c, i], (to, par)))
        return out

    def first_leg(c):
        out = []
        for d, way in enumerate((1, -1)):
            for dz in range(2):
                to = seat(2, dz)
                out.append(remote(
                    x_ref.at[d * (nr // 2) : (d + 1) * (nr // 2), sent(to, c)], relay.at[c, d, dz],
                    a_send.at[c, 5 + 2 * d + dz], a_recv.at[c, 5 + 2 * d + dz], (seat(way, 0), par)))
        return out

    def second_leg(c):
        out = []
        for d, way in enumerate((1, -1)):
            for dz in range(2):
                out.append(remote(
                    relay.at[c, d, dz], landing(seat(-way, 0), d * (nr // 2), nr // 2, c),
                    a_send.at[c, 9 + 2 * d + dz], a_recv.at[c, 9 + 2 * d + dz], (seat(way, dz), par)))
        return out

    def begin(c):
        legs, direct = first_leg(c), straight(c)
        for copy in legs + direct:
            copy.start()
        own = pltpu.make_async_copy(x_ref.at[:, sent(smp, c)], landing(smp, 0, nr, c), own_sem.at[c])
        own.start()
        return legs, direct, own

    def pass_on(c, legs):
        onward = second_leg(c)
        for leg, copy in zip(legs, onward):
            leg.wait_recv()
            copy.start()
        return onward

    scale = 1.0 / np.sqrt(np.float32(total))

    def center(c):
        cols = slice(c * kc, (c + 1) * kc)

        def add(i, acc):
            r = pl.ds(pl.multiple_of(i * 128, 128), 128)
            return acc + jnp.sum(raw[r, cols].astype(jnp.float32).reshape(16, 8, kc), axis=0)

        acc = lax.fori_loop(0, n // 128, add, jnp.zeros((8, kc), jnp.float32))
        mean = jnp.sum(acc, axis=0, keepdims=True) / total

        @pl.loop(0, n // 128)
        def _(i):
            r = pl.ds(pl.multiple_of(i * 128, 128), 128)
            xa[r, cols] = ((raw[r, cols].astype(jnp.float32) - mean) * scale).astype(jnp.bfloat16)

        share = remote(xa.at[:, cols], xp.at[:, cols], share_sem.at[c, 0], share_sem.at[c, 1], partner)
        share.start()
        return share

    def tiles(src, c, first):
        @pl.loop(0, 2 * (nb + 1))
        def _(t):
            a_local = lax.div(t, nb + 1)
            j = lax.rem(t, nb + 1)
            a = core * (nb // 4) + a_local
            tall = j < nb - a
            r = jnp.where(tall, nb - 1 - a, a)
            cb = jnp.where(tall, j, j - (nb - a))
            rows = src[pl.ds(pl.multiple_of(r * B, B), B), c * kc : (c + 1) * kc]
            cols = src[pl.ds(pl.multiple_of(cb * B, B), B), c * kc : (c + 1) * kc]
            got = lax.dot_general(rows, cols, (NT, ((), ())), preferred_element_type=jnp.float32)
            at = (pl.ds(pl.multiple_of(a_local * B, B), B), pl.ds(pl.multiple_of(j * B, B), B))
            F[at] = got if first else F[at] + got

    ebuf[pl.ds(smp, 1)] = en_ref[...][None]
    pl.semaphore_wait(barrier, len(peers))
    shares, moved = [], []
    flight = begin(0)
    for c in range(CHUNKS):
        legs, direct, own = flight
        onward = pass_on(c, legs)
        if c + 1 < CHUNKS:
            flight = begin(c + 1)
        else:
            spread = [remote(en_ref, ebuf.at[smp], e_send.at[d], e_recv.at[d], others[d]) for d in range(7)]
            for copy in spread:
                copy.start()
        for copy in direct + onward:
            copy.wait_recv()
        own.wait()
        moved += legs + direct + onward
        shares.append(center(c))
        tiles(xa, c, c == 0)
        if c > 0:
            shares[c - 1].wait_recv()
            tiles(xp, c - 1, False)
    shares[-1].wait_recv()
    tiles(xp, CHUNKS - 1, False)

    def cols(q):
        return slice(q * width, q * width + width)

    offs = [half - (half >> t) for t in range(STEPS)]
    size = [half >> (t + 1) for t in range(STEPS)]
    base = [[jnp.int32(0)] for q in range(PORTIONS)]

    def halving(t, q):
        who, bit = plans[q][t]
        src = F.at[pl.ds(eight(base[q][t] + (1 - bit) * size[t]), size[t]), cols(q)]
        return remote(src, recv.at[pl.ds(offs[t], size[t]), cols(q)], rs_send.at[t, q], rs_recv.at[t, q], who)

    def accumulate(t, q, start, rows):
        at = (pl.ds(eight(base[q][t + 1] + start), rows), cols(q))
        F[at] += recv[pl.ds(eight(offs[t] + start), rows), cols(q)]

    copies = {}
    for q in range(PORTIONS):
        copies[0, q] = halving(0, q)
        copies[0, q].start()
    for t in range(STEPS):
        for q in range(PORTIONS):
            copies[t, q].wait_recv()
            base[q].append(base[q][t] + plans[q][t][1] * size[t])
            if t + 1 < STEPS:
                bit, s = plans[q][t + 1][1], size[t + 1]
                accumulate(t, q, (1 - bit) * s, s)
                copies[t + 1, q] = halving(t + 1, q)
                copies[t + 1, q].start()
                accumulate(t, q, bit * s, s)
            else:
                accumulate(t, q, 0, size[t])

    def region(row, rows, q):
        return O.at[pl.ds(eight(core * half + row), rows), cols(q)]

    def doubling(t, q):
        here = region(base[q][t + 1], size[t], q)
        return remote(here, here, ag_send.at[t, q], ag_recv.at[t, q], plans[q][t][0])

    def across(t, q, row, rows):
        here = region(row, rows, q)
        return remote(here, here, co_send.at[t, q], co_recv.at[t, q], partner)

    back, forth = {}, []
    for q in range(PORTIONS):
        row, rows = base[q][STEPS], size[STEPS - 1]
        O[pl.ds(eight(core * half + row), rows), cols(q)] = F[pl.ds(eight(row), rows), cols(q)]
        back[STEPS - 1, q] = doubling(STEPS - 1, q)
        back[STEPS - 1, q].start()
        forth.append(across(STEPS, q, row, rows))
        forth[-1].start()
    for t in range(STEPS - 1, -1, -1):
        for q in range(PORTIONS):
            back[t, q].wait_recv()
            if t > 0:
                back[t - 1, q] = doubling(t - 1, q)
                back[t - 1, q].start()
            forth.append(across(t, q, base[q][t] + (1 - plans[q][t][1]) * size[t], size[t]))
            forth[-1].start()
    for copy in shares + moved:
        copy.wait_send()
    for copy in spread:
        copy.wait()
    for copy in [*copies.values(), *back.values()]:
        copy.wait_send()
    for copy in forth:
        copy.wait()


def damped_gram(log_derivs, energy, total):
    n, kp = total, log_derivs.shape[1] // 8
    nr = log_derivs.shape[0]
    nb = n // B
    wide = (nb + 1) * B
    vm = pl.BlockSpec(memory_space=pltpu.VMEM)
    dma = pltpu.SemaphoreType.DMA
    grid = (STEPS, PORTIONS)
    return pl.pallas_call(
        functools.partial(gram_kernel, total),
        out_shape=[
            jax.ShapeDtypeStruct((n // 2, wide), jnp.float32),
            jax.ShapeDtypeStruct((n, kp), jnp.bfloat16),
            jax.ShapeDtypeStruct((8, 8, 128), jnp.float32),
        ],
        in_specs=[pl.BlockSpec(memory_space=pl.ANY), vm],
        out_specs=[vm, vm, vm],
        scratch_shapes=[
            pltpu.VMEM((n // 4, wide), jnp.float32),
            pltpu.VMEM((n // 4, wide), jnp.float32),
            pltpu.VMEM((n, kp), jnp.bfloat16),
            pltpu.VMEM((n, kp), jnp.bfloat16),
            pltpu.VMEM((CHUNKS, 2, 2, nr // 2, kp // CHUNKS), jnp.bfloat16),
            dma((CHUNKS, 2)), dma(grid), dma(grid), dma(grid), dma(grid),
            dma((STEPS + 1, PORTIONS)), dma((STEPS + 1, PORTIONS)), dma((7,)), dma((7,)),
            dma((CHUNKS, 13)), dma((CHUNKS, 13)), dma((CHUNKS,)),
        ],
        compiler_params=pltpu.CompilerParams(
            vmem_limit_bytes=48 * 2**20, collective_id=1, has_side_effects=True
        ),
    )(log_derivs, energy)


def update_kernel(x_ref, xc_ref, u_ref, send, recv):
    smp, par = lax.axis_index("smp"), lax.axis_index("par")
    others = [(lax.rem(smp + d, 8), par) for d in range(1, 8)]
    barrier = pltpu.get_barrier_semaphore()
    for who in others:
        pl.semaphore_signal(barrier, inc=1, device_id=who, device_id_type=MESH)
    hi, lo = split(x_ref[...])
    d = lambda a: lax.dot_general(a, xc_ref[...], (NN, ((), ())), preferred_element_type=jnp.float32)
    term = (d(hi) + d(lo))[0:8]
    u_ref[pl.ds(smp, 1)] = term[None]
    pl.semaphore_wait(barrier, len(others))
    here = u_ref.at[smp]
    copies = [remote(here, here, send.at[i], recv.at[i], others[i]) for i in range(7)]
    for copy in copies:
        copy.start()
    for copy in copies:
        copy.wait()


def project(x, xc):
    vm = pl.BlockSpec(memory_space=pltpu.VMEM)
    u = pl.pallas_call(
        update_kernel,
        out_shape=jax.ShapeDtypeStruct((8, 8, xc.shape[1]), jnp.float32),
        in_specs=[vm, vm],
        out_specs=vm,
        scratch_shapes=[pltpu.SemaphoreType.DMA((7,)), pltpu.SemaphoreType.DMA((7,))],
        compiler_params=pltpu.CompilerParams(
            vmem_limit_bytes=32 * 2**20, collective_id=2, has_side_effects=True
        ),
    )(x, xc)
    return u[:, 0, :].reshape(-1)


SIDE = 10


def local_energy(spins):
    sigma = (2 * spins - 1).astype(jnp.float32).reshape(-1, SIDE, SIDE)
    right = jnp.roll(sigma, 1, axis=2)
    below = jnp.roll(sigma, 1, axis=1)
    diag_one = jnp.roll(below, 1, axis=2)
    diag_two = jnp.roll(below, -1, axis=2)
    nearest = jnp.sum(sigma * right + sigma * below, axis=(1, 2))
    second = jnp.sum(sigma * diag_one + sigma * diag_two, axis=(1, 2))
    return 0.25 * nearest + 0.125 * second


def body(log_derivs, spins, hop_energy):
    rows = log_derivs.shape[0]
    total = rows * 8
    scale = 1.0 / jnp.sqrt(jnp.float32(total))
    energy = local_energy(spins) + hop_energy
    energy = jnp.pad(energy.reshape(rows // 128, 128), ((0, 8 - rows // 128), (0, 0)))
    gram, centered, energies = damped_gram(log_derivs, energy, total)
    all_energy = energies[:, : rows // 128].reshape(-1)
    eps = (all_energy - jnp.mean(all_energy)) * scale
    coeffs = solve(gram, eps)
    update = project(coeffs, centered)
    start = lax.axis_index("smp") * rows
    return update, lax.dynamic_slice_in_dim(coeffs[0], start, rows, 0)


def solution(mesh):
    placed = (P("smp", "par"), P("smp", None), P("smp"))
    return jax.shard_map(
        body, mesh=mesh, in_specs=placed, out_specs=(P("par"), P("smp")), check_vma=False
    )
```

```python
import functools
import jax, jax.numpy as jnp
import numpy as np
from jax import lax
from jax.experimental import pallas as pl
from jax.experimental.pallas import tpu as pltpu
from jax.sharding import PartitionSpec as P

B = 256
H = 128
NT = ((1,), (1,))
NN = ((1,), (0,))


def split(x):
    hi = x.astype(jnp.bfloat16)
    return hi, (x - hi.astype(jnp.float32)).astype(jnp.bfloat16)


def dot3(ah, al, bh, bl, dims):
    d = lambda a, b: lax.dot_general(a, b, (dims, ((), ())), preferred_element_type=jnp.float32)
    return d(ah, bh) + (d(ah, bl) + d(al, bh))


def splat(x):
    return jnp.broadcast_to(x, (8, H))


def factor_inverse(groups, T, R, A2, beside):
    lane = lax.broadcasted_iota(jnp.int32, (8, H), 1)
    sub = lax.broadcasted_iota(jnp.int32, (8, H), 0)
    out = []
    corner = [splat(groups[0][:, j : j + 1]) for j in range(8)]
    for p in range(16):
        if beside is not None:
            beside(p)
        lo, slot = 8 * p, p % 2
        pivots, at = groups[p], 64 * slot
        for j in range(8):
            T[at + 8 * j : at + 8 * j + 8, :] = corner[j]
        inside = (lane >= lo) & (lane < lo + 8)
        R[8 * slot : 8 * slot + 8, :] = jnp.where(inside, (lane - lo == sub).astype(jnp.float32), pivots)
        e = {}
        for j in range(8):
            for i in range(j, 8):
                e[i, j] = splat(T[at + 8 * j + i : at + 8 * j + i + 1, :])
        y = [splat(R[8 * slot + i : 8 * slot + i + 1, :]) for i in range(8)]
        last = p == 15
        if not last:
            near = groups[p + 1]
            a = [splat(near[:, lo + j : lo + j + 1]) for j in range(8)]
            corner = [splat(near[:, lo + 8 + j : lo + 9 + j]) for j in range(8)]
            near = jnp.where(inside, 0.0, near)
        m, r, u = {}, [], None
        for k in range(8):
            rk = pl.reciprocal(e[k, k], approx=True)
            r.append(rk)
            for i in range(k + 1, 8):
                m[i, k] = e[i, k] * rk
            for i in range(k + 1, 8):
                for q in range(k + 1, i + 1):
                    if i == q == k + 1:
                        e[i, q] = e[i, q] - (e[i, k] * e[i, k]) * rk
                    else:
                        e[i, q] = e[i, q] - m[i, k] * e[q, k]
            for i in range(k + 1, 8):
                y[i] = y[i] - m[i, k] * y[k]
            row = y[k] * lax.rsqrt(e[k, k])
            u = row if k == 0 else jnp.where(sub == k, row, u)
            if not last:
                for i in range(k + 1, 8):
                    a[i] = a[i] - m[i, k] * a[k]
                scaled = a[k] * rk
                A2[at + 8 * k : at + 8 * k + 8, :] = scaled
                near = near - scaled * y[k]
                for j in range(8):
                    corner[j] = corner[j] - a[k] * splat(A2[at + 8 * k + j : at + 8 * k + j + 1, :])
        out.append(u)
        if last:
            break
        groups[p + 1] = near
        v = [None] * 8
        for j in range(7, -1, -1):
            t = r[j] * y[j]
            for k in range(7, j, -1):
                t = t - m[k, j] * v[k]
            v[j] = t
        for g in range(p + 2, 16):
            old = groups[g]
            t = [splat(old[:, lo + j : lo + j + 1]) * v[j] for j in range(8)]
            t = ((t[0] + t[1]) + (t[2] + t[3])) + ((t[4] + t[5]) + (t[6] + t[7]))
            groups[g] = jnp.where(inside, 0.0, old) - t
    return [jnp.where(lane <= sub + 8 * g, out[g], 0.0) for g in range(16)]


def slot(nb, i, k):
    return nb * k - lax.div(k * (k - 1), 2) + i - k


def tile(nb, i, k):
    t = slot(nb, i, k)
    a, j = lax.rem(t, PACK), lax.div(t, PACK)
    return lax.div(j, 3), 2 * lax.rem(j, 3), pl.multiple_of(a * B, B)


def get(G, at):
    s, q, r = at
    return jnp.concatenate([G[s, q, pl.ds(r, B), :], G[s, q + 1, pl.ds(r, B), :]], axis=1)


def put(G, at, value):
    s, q, r = at
    G[s, q, pl.ds(r, B), :] = value[:, 0:H]
    G[s, q + 1, pl.ds(r, B), :] = value[:, H:B]


def sub(G, at, value):
    s, q, r = at
    G[s, q, pl.ds(r, B), :] -= value[:, 0:H]
    G[s, q + 1, pl.ds(r, B), :] -= value[:, H:B]


def block(i):
    return pl.ds(pl.multiple_of(i * B, B), B)


SLOTS = 8
PACK = 4


def kernel(n, g_ref, e_ref, x_ref, G, lhi, llo, ec, whi, wlo, D, W, T, R, A2, z, sem):
    nb = n // B
    load = pltpu.make_async_copy(g_ref, G.at[:, :, 0 : n // 2, :], sem)
    load.start()
    ec[...] = e_ref[...]
    diag = lax.broadcasted_iota(jnp.int32, (H, H), 0) == lax.broadcasted_iota(jnp.int32, (H, H), 1)
    damp = jnp.where(diag, jnp.float32(0.2), jnp.float32(0.0))
    load.wait()

    def triangle(k, i):
        ch, cl = split(get(G, tile(nb, i, k)))
        th, tl = split(dot3(ch, cl, whi[k], wlo[k], NT))
        lhi[block(i), block(k)], llo[block(i), block(k)] = th, tl
        yh, yl = split(z[:, block(k)])
        ec[:, block(i)] -= dot3(yh, yl, th, tl, NT)
        return th, tl

    def factor(k, h, slots):
        def beside(p):
            if p % (16 // SLOTS) != 0:
                return
            s = h * SLOTS + p // (16 // SLOTS)
            live = s < (k + 1) * (nb - 1 - k)
            i = jnp.minimum(k + 1 + lax.div(s, k + 1), nb - 1)
            u = lax.rem(s, k + 1)
            own = u == k
            column = jnp.where(own, k, jnp.minimum(k + 1, nb - 1))
            j = jnp.where(own, k - 1, u)
            at = tile(nb, i, column)
            at = (at[0], at[1], pl.multiple_of(jnp.where(live, at[2], n // 2), B))
            sub(G, at, dot3(
                lhi[block(i), block(j)], llo[block(i), block(j)],
                lhi[block(column), block(j)], llo[block(column), block(j)], NT))

        got = factor_inverse([D[8 * g : 8 * g + 8, :] for g in range(16)], T, R, A2, beside if slots else None)
        for g in range(16):
            W[h, 8 * g : 8 * g + 8, :] = got[g]

    def chain(k, h):
        some = (k > 0) & (k < nb - 1)

        @pl.when(some)
        def _():
            factor(k, h, True)

        @pl.when(jnp.logical_not(some))
        def _():
            factor(k, h, False)

    def panel(k, _):
        home = tile(nb, k, k)

        @pl.when(k > 0)
        def _():
            th, tl = triangle(k - 1, k)
            sub(G, home, dot3(th, tl, th, tl, NT))

            @pl.loop(k + 1, nb)
            def _(i):
                triangle(k - 1, i)

        hs, hq, hr = home
        top, low = pl.ds(hr, H), pl.ds(pl.multiple_of(hr + H, H), H)
        D[...] = G[hs, hq, top, :] + damp
        chain(k, 0)
        w1h, w1l = split(W[0])
        ah, al = split(G[hs, hq, low, :])
        lh, ll = split(dot3(ah, al, w1h, w1l, NT))
        D[...] = G[hs, hq + 1, low, :] + damp - dot3(lh, ll, lh, ll, NT)
        th, tl = split(dot3(lh, ll, w1h, w1l, NN))
        whi[k, 0:H, 0:H], wlo[k, 0:H, 0:H] = w1h, w1l
        whi[k, 0:H, H:B] = jnp.zeros((H, H), jnp.bfloat16)
        wlo[k, 0:H, H:B] = jnp.zeros((H, H), jnp.bfloat16)
        chain(k, 1)
        w2h, w2l = split(W[1])
        whi[k, H:B, H:B], wlo[k, H:B, H:B] = w2h, w2l
        whi[k, H:B, 0:H], wlo[k, H:B, 0:H] = split(-dot3(w2h, w2l, th, tl, NN))
        eh, el = split(ec[:, block(k)])
        z[:, block(k)] = dot3(eh, el, whi[k], wlo[k], NT)
        return 0

    lax.fori_loop(0, nb, panel, 0)
    for kk in range(nb - 1, -1, -1):
        cols = slice(kk * B, kk * B + B)
        zh, zl = split(z[:, cols])
        x = dot3(zh, zl, whi[kk], wlo[kk], NN)
        x_ref[:, cols] = x
        if kk > 0:
            xh, xl = split(x)
            z[:, : kk * B] -= dot3(xh, xl, lhi[cols, : kk * B], llo[cols, : kk * B], NN)


def solve(a, eps):
    n = eps.shape[0]
    e = jnp.zeros((16, n), jnp.float32).at[0].set(eps)
    nb = n // B
    vm = pl.BlockSpec(memory_space=pltpu.VMEM)
    return pl.pallas_call(
        functools.partial(kernel, n),
        out_shape=jax.ShapeDtypeStruct((16, n), jnp.float32),
        in_specs=[pl.BlockSpec(memory_space=pl.ANY), vm],
        out_specs=vm,
        scratch_shapes=[
            pltpu.VMEM((3, 6, n // 2 + B, H), jnp.float32),
            pltpu.VMEM((n, n), jnp.bfloat16),
            pltpu.VMEM((n, n), jnp.bfloat16),
            pltpu.VMEM((16, n), jnp.float32),
            pltpu.VMEM((nb, B, B), jnp.bfloat16),
            pltpu.VMEM((nb, B, B), jnp.bfloat16),
            pltpu.VMEM((H, H), jnp.float32),
            pltpu.VMEM((2, H, H), jnp.float32),
            pltpu.VMEM((128, H), jnp.float32),
            pltpu.VMEM((16, H), jnp.float32),
            pltpu.VMEM((128, H), jnp.float32),
            pltpu.VMEM((16, n), jnp.float32),
            pltpu.SemaphoreType.DMA,
        ],
        compiler_params=pltpu.CompilerParams(vmem_limit_bytes=56 * 2**20),
    )(a, e)


MESH = pl.DeviceIdType.MESH
PORTIONS = 6
CHUNKS = 2


def place():
    smp, par = lax.axis_index("smp"), lax.axis_index("par")
    y, z_lo = lax.div(smp, 2), lax.rem(smp, 2)
    x, z_hi, core = lax.div(par, 4), lax.rem(lax.div(par, 2), 2), lax.rem(par, 2)
    return (x, y, z_hi * 2 + z_lo), core


def device(pos, core):
    x, y, z = pos
    return (y * 2 + lax.rem(z, 2), x * 4 + lax.div(z, 2) * 2 + core)


def plan(pos, core, q):
    first = q // 2

    def at(axis, i):
        there = list(pos)
        there[axis] = i
        return device(there, core)

    i = pos[first]
    low, high = lax.rem(i, 2), lax.div(i, 2)
    near, far = at(first, i + 1 - 2 * low), at(first, 3 - i)
    if q % 2 == 0:
        halves = [(near, lax.rem(low + high, 2)), (far, high)]
    else:
        halves = [(far, high), (near, low)]
    cuts = []
    for stage in (1, 2):
        axis = (first + stage) % 3
        cuts.append((pos[axis], [at(axis, lax.rem(pos[axis] + d, 4)) for d in (1, 2, 3)]))
    return halves, cuts


def remote(src, dst, send, recv, who):
    return pltpu.make_async_remote_copy(
        src_ref=src, dst_ref=dst, send_sem=send, recv_sem=recv, device_id=who, device_id_type=MESH
    )


def eight(x):
    return pl.multiple_of(x, 8)


def gram_kernel(total, x_ref, en_ref, O, xa, ebuf, F, recv, raw, xp, relay,
                share_sem, c_send, c_recv, e_send, e_recv,
                a_send, a_recv, own_sem):
    pos, core = place()
    smp, par = lax.axis_index("smp"), lax.axis_index("par")
    n, kp = raw.shape
    nr = x_ref.shape[0]
    kc = kp // CHUNKS
    nb = n // B
    half = F.shape[2]
    plans = [plan(pos, core, q) for q in range(PORTIONS)]
    partner = device(pos, 1 - core)
    others = [(lax.rem(smp + d, 8), par) for d in range(1, 8)]
    peers = [partner] + [who for q in (0, 2, 4) for who in plans[q][1][0][1]] + others
    barrier = pltpu.get_barrier_semaphore()
    for who in peers:
        pl.semaphore_signal(barrier, inc=1, device_id=who, device_id_type=MESH)

    y, z_lo = lax.div(smp, 2), lax.rem(smp, 2)

    def seat(dy, dz):
        return lax.rem(y + dy + 4, 4) * 2 + (1 - z_lo if dz else z_lo)

    def sent(to, c):
        return pl.ds(pl.multiple_of(to * kp + c * kc, kc), kc)

    def landing(origin, row, rows, c):
        return raw.at[pl.ds(pl.multiple_of(origin * nr + row, rows), rows), c * kc : (c + 1) * kc]

    def straight(c):
        out = []
        for i, (dy, dz) in enumerate([(1, 0), (-1, 0), (1, 1), (-1, 1), (0, 1)]):
            to = seat(dy, dz)
            out.append(remote(x_ref.at[:, sent(to, c)], landing(smp, 0, nr, c), a_send.at[c, i], a_recv.at[c, i], (to, par)))
        return out

    def first_leg(c):
        out = []
        for d, way in enumerate((1, -1)):
            for dz in range(2):
                to = seat(2, dz)
                out.append(remote(
                    x_ref.at[d * (nr // 2) : (d + 1) * (nr // 2), sent(to, c)], relay.at[c, d, dz],
                    a_send.at[c, 5 + 2 * d + dz], a_recv.at[c, 5 + 2 * d + dz], (seat(way, 0), par)))
        return out

    def second_leg(c):
        out = []
        for d, way in enumerate((1, -1)):
            for dz in range(2):
                out.append(remote(
                    relay.at[c, d, dz], landing(seat(-way, 0), d * (nr // 2), nr // 2, c),
                    a_send.at[c, 9 + 2 * d + dz], a_recv.at[c, 9 + 2 * d + dz], (seat(way, dz), par)))
        return out

    def begin(c):
        legs, direct = first_leg(c), straight(c)
        for copy in legs + direct:
            copy.start()
        own = pltpu.make_async_copy(x_ref.at[:, sent(smp, c)], landing(smp, 0, nr, c), own_sem.at[c])
        own.start()
        return legs, direct, own

    def pass_on(c, legs):
        onward = second_leg(c)
        for leg, copy in zip(legs, onward):
            leg.wait_recv()
            copy.start()
        return onward

    scale = 1.0 / np.sqrt(np.float32(total))

    def center(c):
        cols = slice(c * kc, (c + 1) * kc)

        def add(i, acc):
            r = pl.ds(pl.multiple_of(i * 128, 128), 128)
            return acc + jnp.sum(raw[r, cols].astype(jnp.float32).reshape(16, 8, kc), axis=0)

        acc = lax.fori_loop(0, n // 128, add, jnp.zeros((8, kc), jnp.float32))
        mean = jnp.sum(acc, axis=0, keepdims=True) / total

        @pl.loop(0, n // 128)
        def _(i):
            r = pl.ds(pl.multiple_of(i * 128, 128), 128)
            xa[r, cols] = ((raw[r, cols].astype(jnp.float32) - mean) * scale).astype(jnp.bfloat16)

        share = remote(xa.at[:, cols], xp.at[:, cols], share_sem.at[c, 0], share_sem.at[c, 1], partner)
        share.start()
        return share

    starts = [nb * k - k * (k - 1) // 2 for k in range(1, nb)]

    def tiles(src, c, first):
        @pl.loop(0, 2 * (nb + 1))
        def _(it):
            a_local, j = lax.rem(it, 2), lax.div(it, 2)
            t = PACK * j + 2 * core + a_local
            k = sum(jnp.where(t >= start, 1, 0) for start in starts)
            i = t - (nb * k - lax.div(k * (k - 1), 2)) + k
            rows = src[block(i), c * kc : (c + 1) * kc]
            cols = src[block(k), c * kc : (c + 1) * kc]
            got = lax.dot_general(rows, cols, (NT, ((), ())), preferred_element_type=jnp.float32)
            at = (lax.div(j, 3), 2 * lax.rem(j, 3), pl.multiple_of(a_local * B, B))
            put(F, at, got if first else get(F, at) + got)

    ebuf[pl.ds(smp, 1)] = en_ref[...][None]
    pl.semaphore_wait(barrier, len(peers))
    shares, moved = [], []
    spread = [remote(en_ref, ebuf.at[smp], e_send.at[d], e_recv.at[d], others[d]) for d in range(7)]
    flight = begin(0)
    for c in range(CHUNKS):
        legs, direct, own = flight
        onward = pass_on(c, legs)
        if c + 1 < CHUNKS:
            flight = begin(c + 1)
        else:
            for copy in spread:
                copy.start()
        for copy in direct + onward:
            copy.wait_recv()
        own.wait()
        moved += legs + direct + onward
        shares.append(center(c))
        tiles(xa, c, c == 0)
        shares[c].wait_recv()
        tiles(xp, c, False)
    portions = range(PORTIONS)
    base = []
    for q in portions:
        rows, at = half, jnp.int32(0)
        base.append([at])
        for _, bit in plans[q][0]:
            rows = rows // 2
            at = at + bit * rows
            base[q].append(at)
        for i, _ in plans[q][1]:
            rows = rows // 4
            at = at + i * rows
            base[q].append(at)
    size = [half, half // 2, half // 4, half // 16, half // 64]
    offs = [0, size[1], size[1] + size[2], size[1] + size[2] + 3 * size[3]]

    def part(ref, q, row, rows):
        return ref.at[:, q, pl.ds(eight(row), rows), :]

    def accumulate(q, row, rows, held):
        at = (slice(None), q, pl.ds(eight(row), rows), slice(None))
        F[at] += recv[:, q, pl.ds(eight(held), rows), :]

    sem = iter(range(10**6))
    pending = []

    def go(src, dst, who):
        i = next(sem)
        copy = remote(src, dst, c_send.at[i], c_recv.at[i], who)
        copy.start()
        pending.append(copy)
        return copy

    def halve(q, t):
        who, bit = plans[q][0][t]
        row = base[q][t] + (1 - bit) * size[t + 1]
        return go(part(F, q, row, size[t + 1]), part(recv, q, offs[t], size[t + 1]), who)

    def cut(q, stage):
        i, whos = plans[q][1][stage]
        rows = size[stage + 3]
        out = []
        for d, who in enumerate(whos):
            row = base[q][stage + 2] + lax.rem(i + d + 1, 4) * rows
            out.append(go(part(F, q, row, rows), part(recv, q, offs[stage + 2] + d * rows, rows), who))
        return out

    one = [halve(q, 0) for q in portions]
    two, three, four = [], [], []
    for q in portions:
        one[q].wait_recv()
        bit, rows = plans[q][0][1][1], size[2]
        accumulate(q, base[q][1] + (1 - bit) * rows, rows, offs[0] + (1 - bit) * rows)
        two.append(halve(q, 1))
        accumulate(q, base[q][2], rows, offs[0] + bit * rows)
    for q in portions:
        two[q].wait_recv()
        accumulate(q, base[q][2], size[2], offs[1])
        three.append(cut(q, 0))
    for q in portions:
        for d, copy in enumerate(three[q]):
            copy.wait_recv()
            accumulate(q, base[q][3], size[3], offs[2] + d * size[3])
        four.append(cut(q, 1))
    for q in portions:
        for d, copy in enumerate(four[q]):
            copy.wait_recv()
            accumulate(q, base[q][4], size[4], offs[3] + d * size[4])
        at = pl.ds(eight(core * half + base[q][4]), size[4])
        O[:, q, at, :] = F[:, q, pl.ds(eight(base[q][4]), size[4]), :]
    def region(q, row, rows):
        return part(O, q, core * half + row, rows)

    def spread_out(q, stage):
        here = region(q, base[q][stage + 3], size[stage + 3])
        return [go(here, here, who) for who in plans[q][1][stage][1]]

    def double(q, t):
        here = region(q, base[q][t + 1], size[t + 1])
        return go(here, here, plans[q][0][t][0])

    def across(q, row):
        here = region(q, row, size[1])
        return go(here, here, partner)

    five, six, seven, eighth, over = [], [], [], [], []
    for q in portions:
        five.append(spread_out(q, 1))
    for q in portions:
        for copy in five[q]:
            copy.wait_recv()
        six.append(spread_out(q, 0))
    for q in portions:
        for copy in six[q]:
            copy.wait_recv()
        seven.append(double(q, 1))
    for q in portions:
        seven[q].wait_recv()
        eighth.append(double(q, 0))
        over.append(across(q, base[q][1]))
    for q in portions:
        eighth[q].wait_recv()
        over.append(across(q, size[1] - base[q][1]))
    for copy in over:
        copy.wait_recv()
    for copy in pending:
        copy.wait_send()
    for copy in spread:
        copy.wait()
    for copy in shares + moved:
        copy.wait_send()


def damped_gram(log_derivs, energy, total):
    n, kp = total, log_derivs.shape[1] // 8
    nr = log_derivs.shape[0]
    vm = pl.BlockSpec(memory_space=pltpu.VMEM)
    dma = pltpu.SemaphoreType.DMA
    return pl.pallas_call(
        functools.partial(gram_kernel, total),
        out_shape=[
            jax.ShapeDtypeStruct((3, PORTIONS, n // 2, H), jnp.float32),
            jax.ShapeDtypeStruct((n, kp), jnp.bfloat16),
            jax.ShapeDtypeStruct((8, 8, 128), jnp.float32),
        ],
        in_specs=[pl.BlockSpec(memory_space=pl.ANY), vm],
        out_specs=[vm, vm, vm],
        scratch_shapes=[
            pltpu.VMEM((3, PORTIONS, n // 4, H), jnp.float32),
            pltpu.VMEM((3, PORTIONS, n // 4, H), jnp.float32),
            pltpu.VMEM((n, kp), jnp.bfloat16),
            pltpu.VMEM((n, kp), jnp.bfloat16),
            pltpu.VMEM((CHUNKS, 2, 2, nr // 2, kp // CHUNKS), jnp.bfloat16),
            dma((CHUNKS, 2)), dma((18 * PORTIONS,)), dma((18 * PORTIONS,)), dma((7,)), dma((7,)),
            dma((CHUNKS, 13)), dma((CHUNKS, 13)), dma((CHUNKS,)),
        ],
        compiler_params=pltpu.CompilerParams(
            vmem_limit_bytes=48 * 2**20, collective_id=1, has_side_effects=True
        ),
    )(log_derivs, energy)


def update_kernel(x_ref, xc_ref, u_ref, send, recv):
    smp, par = lax.axis_index("smp"), lax.axis_index("par")
    others = [(lax.rem(smp + d, 8), par) for d in range(1, 8)]
    barrier = pltpu.get_barrier_semaphore()
    for who in others:
        pl.semaphore_signal(barrier, inc=1, device_id=who, device_id_type=MESH)
    hi, lo = split(x_ref[...])
    d = lambda a: lax.dot_general(a, xc_ref[...], (NN, ((), ())), preferred_element_type=jnp.float32)
    term = (d(hi) + d(lo))[0:8]
    u_ref[pl.ds(smp, 1)] = term[None]
    pl.semaphore_wait(barrier, len(others))
    here = u_ref.at[smp]
    copies = [remote(here, here, send.at[i], recv.at[i], others[i]) for i in range(7)]
    for copy in copies:
        copy.start()
    for copy in copies:
        copy.wait()


def project(x, xc):
    vm = pl.BlockSpec(memory_space=pltpu.VMEM)
    u = pl.pallas_call(
        update_kernel,
        out_shape=jax.ShapeDtypeStruct((8, 8, xc.shape[1]), jnp.float32),
        in_specs=[vm, vm],
        out_specs=vm,
        scratch_shapes=[pltpu.SemaphoreType.DMA((7,)), pltpu.SemaphoreType.DMA((7,))],
        compiler_params=pltpu.CompilerParams(
            vmem_limit_bytes=32 * 2**20, collective_id=2, has_side_effects=True
        ),
    )(x, xc)
    return u[:, 0, :].reshape(-1)


SIDE = 10


def local_energy(spins):
    sigma = (2 * spins - 1).astype(jnp.float32).reshape(-1, SIDE, SIDE)
    right = jnp.roll(sigma, 1, axis=2)
    below = jnp.roll(sigma, 1, axis=1)
    diag_one = jnp.roll(below, 1, axis=2)
    diag_two = jnp.roll(below, -1, axis=2)
    nearest = jnp.sum(sigma * right + sigma * below, axis=(1, 2))
    second = jnp.sum(sigma * diag_one + sigma * diag_two, axis=(1, 2))
    return 0.25 * nearest + 0.125 * second


def body(log_derivs, spins, hop_energy):
    rows = log_derivs.shape[0]
    total = rows * 8
    scale = 1.0 / jnp.sqrt(jnp.float32(total))
    energy = local_energy(spins) + hop_energy
    energy = jnp.pad(energy.reshape(rows // 128, 128), ((0, 8 - rows // 128), (0, 0)))
    gram, centered, energies = damped_gram(log_derivs, energy, total)
    all_energy = energies[:, : rows // 128].reshape(-1)
    eps = (all_energy - jnp.mean(all_energy)) * scale
    coeffs = solve(gram, eps)
    update = project(coeffs, centered)
    start = lax.axis_index("smp") * rows
    return update, lax.dynamic_slice_in_dim(coeffs[0], start, rows, 0)


def solution(mesh):
    placed = (P("smp", "par"), P("smp", None), P("smp"))
    return jax.shard_map(
        body, mesh=mesh, in_specs=placed, out_specs=(P("par"), P("smp")), check_vma=False
    )
```

```python
import functools
import jax, jax.numpy as jnp
import numpy as np
from jax import lax
from jax.experimental import pallas as pl
from jax.experimental.pallas import tpu as pltpu
from jax.sharding import PartitionSpec as P

B = 256
H = 128
NT = ((1,), (1,))
NN = ((1,), (0,))


def split(x):
    hi = x.astype(jnp.bfloat16)
    return hi, (x - hi.astype(jnp.float32)).astype(jnp.bfloat16)


def dot3(ah, al, bh, bl, dims):
    d = lambda a, b: lax.dot_general(a, b, (dims, ((), ())), preferred_element_type=jnp.float32)
    return d(ah, bh) + (d(ah, bl) + d(al, bh))


def splat(x):
    return jnp.broadcast_to(x, (8, H))


def factor_inverse(groups, T, R, A2, beside):
    lane = lax.broadcasted_iota(jnp.int32, (8, H), 1)
    sub = lax.broadcasted_iota(jnp.int32, (8, H), 0)
    out = []
    corner = [splat(groups[0][:, j : j + 1]) for j in range(8)]
    for p in range(16):
        if beside is not None:
            beside(p)
        lo, slot = 8 * p, p % 2
        pivots, at = groups[p], 64 * slot
        for j in range(8):
            T[at + 8 * j : at + 8 * j + 8, :] = corner[j]
        inside = (lane >= lo) & (lane < lo + 8)
        R[8 * slot : 8 * slot + 8, :] = jnp.where(inside, (lane - lo == sub).astype(jnp.float32), pivots)
        e = {}
        for j in range(8):
            for i in range(j, 8):
                e[i, j] = splat(T[at + 8 * j + i : at + 8 * j + i + 1, :])
        y = [splat(R[8 * slot + i : 8 * slot + i + 1, :]) for i in range(8)]
        last = p == 15
        if not last:
            near = groups[p + 1]
            a = [splat(near[:, lo + j : lo + j + 1]) for j in range(8)]
            corner = [splat(near[:, lo + 8 + j : lo + 9 + j]) for j in range(8)]
            near = jnp.where(inside, 0.0, near)
        m, r, u = {}, [], None
        for k in range(8):
            rk = pl.reciprocal(e[k, k], approx=True)
            r.append(rk)
            for i in range(k + 1, 8):
                m[i, k] = e[i, k] * rk
            for i in range(k + 1, 8):
                for q in range(k + 1, i + 1):
                    if i == q == k + 1:
                        e[i, q] = e[i, q] - (e[i, k] * e[i, k]) * rk
                    else:
                        e[i, q] = e[i, q] - m[i, k] * e[q, k]
            for i in range(k + 1, 8):
                y[i] = y[i] - m[i, k] * y[k]
            row = y[k] * lax.rsqrt(e[k, k])
            u = row if k == 0 else jnp.where(sub == k, row, u)
            if not last:
                for i in range(k + 1, 8):
                    a[i] = a[i] - m[i, k] * a[k]
                scaled = a[k] * rk
                A2[at + 8 * k : at + 8 * k + 8, :] = scaled
                near = near - scaled * y[k]
                for j in range(8):
                    corner[j] = corner[j] - a[k] * splat(A2[at + 8 * k + j : at + 8 * k + j + 1, :])
        out.append(u)
        if last:
            break
        groups[p + 1] = near
        v = [None] * 8
        for j in range(7, -1, -1):
            t = r[j] * y[j]
            for k in range(7, j, -1):
                t = t - m[k, j] * v[k]
            v[j] = t
        for g in range(p + 2, 16):
            old = groups[g]
            t = [splat(old[:, lo + j : lo + j + 1]) * v[j] for j in range(8)]
            t = ((t[0] + t[1]) + (t[2] + t[3])) + ((t[4] + t[5]) + (t[6] + t[7]))
            groups[g] = jnp.where(inside, 0.0, old) - t
    return [jnp.where(lane <= sub + 8 * g, out[g], 0.0) for g in range(16)]


def slot(nb, i, k):
    return nb * k - lax.div(k * (k - 1), 2) + i - k


def tile(nb, i, k):
    t = slot(nb, i, k)
    a, j = lax.rem(t, PACK), lax.div(t, PACK)
    return lax.div(j, 3), 2 * lax.rem(j, 3), pl.multiple_of(a * B, B)


def get(G, at):
    s, q, r = at
    return jnp.concatenate([G[s, q, pl.ds(r, B), :], G[s, q + 1, pl.ds(r, B), :]], axis=1)


def put(G, at, value):
    s, q, r = at
    G[s, q, pl.ds(r, B), :] = value[:, 0:H]
    G[s, q + 1, pl.ds(r, B), :] = value[:, H:B]


def sub(G, at, value):
    s, q, r = at
    G[s, q, pl.ds(r, B), :] -= value[:, 0:H]
    G[s, q + 1, pl.ds(r, B), :] -= value[:, H:B]


def block(i):
    return pl.ds(pl.multiple_of(i * B, B), B)


SLOTS = 8
PACK = 4


def solve(n, x_ref, G, lhi, llo, ec, whi, wlo, D, W, T, R, A2, z, hooks):
    nb = n // B
    diag = lax.broadcasted_iota(jnp.int32, (H, H), 0) == lax.broadcasted_iota(jnp.int32, (H, H), 1)
    damp = jnp.where(diag, jnp.float32(0.2), jnp.float32(0.0))

    def span(k):
        return slice(k * B, k * B + B) if isinstance(k, int) else block(k)

    def triangle(k, i):
        ch, cl = split(get(G, tile(nb, i, k)))
        th, tl = split(dot3(ch, cl, whi[k], wlo[k], NT))
        lhi[block(i), span(k)], llo[block(i), span(k)] = th, tl
        yh, yl = split(z[:, span(k)])
        ec[:, block(i)] -= dot3(yh, yl, th, tl, NT)
        return th, tl

    def factor(k, h, slots):
        def beside(p):
            if p % (16 // SLOTS) != 0:
                return
            s = h * SLOTS + p // (16 // SLOTS)
            live = s < (k + 1) * (nb - 1 - k)
            i = jnp.minimum(k + 1 + lax.div(s, k + 1), nb - 1)
            u = lax.rem(s, k + 1)
            own = u == k
            column = jnp.where(own, k, jnp.minimum(k + 1, nb - 1))
            j = jnp.where(own, k - 1, u)
            at = tile(nb, i, column)
            at = (at[0], at[1], pl.multiple_of(jnp.where(live, at[2], n // 2), B))
            sub(G, at, dot3(
                lhi[block(i), block(j)], llo[block(i), block(j)],
                lhi[block(column), block(j)], llo[block(column), block(j)], NT))

        got = factor_inverse([D[8 * g : 8 * g + 8, :] for g in range(16)], T, R, A2, beside if slots else None)
        for g in range(16):
            W[h, 8 * g : 8 * g + 8, :] = got[g]

    def chain(k, h):
        if isinstance(k, int):
            factor(k, h, False)
            return

        @pl.when(k < nb - 1)
        def _():
            factor(k, h, True)

        @pl.when(k == nb - 1)
        def _():
            factor(k, h, False)

    def panel(k):
        first = isinstance(k, int)
        home = (0, 0, 0) if first else tile(nb, k, k)
        if not first:
            th, tl = triangle(k - 1, k)
            sub(G, home, dot3(th, tl, th, tl, NT))

            @pl.loop(k + 1, nb)
            def _(i):
                triangle(k - 1, i)

        hs, hq, hr = home
        top, low = (pl.ds(0, H), pl.ds(H, H)) if first else (pl.ds(hr, H), pl.ds(pl.multiple_of(hr + H, H), H))
        D[...] = G[hs, hq, top, :] + damp
        if first:
            hooks[0]()
        chain(k, 0)
        if first:
            hooks[1]()
        w1h, w1l = split(W[0])
        ah, al = split(G[hs, hq, low, :])
        lh, ll = split(dot3(ah, al, w1h, w1l, NT))
        D[...] = G[hs, hq + 1, low, :] + damp - dot3(lh, ll, lh, ll, NT)
        th, tl = split(dot3(lh, ll, w1h, w1l, NN))
        whi[k, 0:H, 0:H], wlo[k, 0:H, 0:H] = w1h, w1l
        whi[k, 0:H, H:B] = jnp.zeros((H, H), jnp.bfloat16)
        wlo[k, 0:H, H:B] = jnp.zeros((H, H), jnp.bfloat16)
        chain(k, 1)
        if first:
            hooks[2]()
        w2h, w2l = split(W[1])
        whi[k, H:B, H:B], wlo[k, H:B, H:B] = w2h, w2l
        whi[k, H:B, 0:H], wlo[k, H:B, 0:H] = split(-dot3(w2h, w2l, th, tl, NN))
        eh, el = split(ec[:, span(k)])
        z[:, span(k)] = dot3(eh, el, whi[k], wlo[k], NT)

    panel(0)

    @pl.loop(1, nb)
    def _(k):
        @pl.when(k == 1)
        def _():
            hooks[3]()

        panel(k)

    for kk in range(nb - 1, -1, -1):
        cols = slice(kk * B, kk * B + B)
        zh, zl = split(z[:, cols])
        x = dot3(zh, zl, whi[kk], wlo[kk], NN)
        x_ref[:, cols] = x
        if kk > 0:
            xh, xl = split(x)
            z[:, : kk * B] -= dot3(xh, xl, lhi[cols, : kk * B], llo[cols, : kk * B], NN)


MESH = pl.DeviceIdType.MESH
PORTIONS = 6
CHUNKS = 2


def place():
    smp, par = lax.axis_index("smp"), lax.axis_index("par")
    y, z_lo = lax.div(smp, 2), lax.rem(smp, 2)
    x, z_hi, core = lax.div(par, 4), lax.rem(lax.div(par, 2), 2), lax.rem(par, 2)
    return (x, y, z_hi * 2 + z_lo), core


def device(pos, core):
    x, y, z = pos
    return (y * 2 + lax.rem(z, 2), x * 4 + lax.div(z, 2) * 2 + core)


def plan(pos, core, q):
    first = q // 2

    def at(axis, i):
        there = list(pos)
        there[axis] = i
        return device(there, core)

    i = pos[first]
    low, high = lax.rem(i, 2), lax.div(i, 2)
    near, far = at(first, i + 1 - 2 * low), at(first, 3 - i)
    if q % 2 == 0:
        halves = [(near, lax.rem(low + high, 2)), (far, high)]
    else:
        halves = [(far, high), (near, low)]
    cuts = []
    for stage in (1, 2):
        axis = (first + stage) % 3
        cuts.append((pos[axis], [at(axis, lax.rem(pos[axis] + d, 4)) for d in (1, 2, 3)]))
    return halves, cuts


def remote(src, dst, send, recv, who):
    return pltpu.make_async_remote_copy(
        src_ref=src, dst_ref=dst, send_sem=send, recv_sem=recv, device_id=who, device_id_type=MESH
    )


def eight(x):
    return pl.multiple_of(x, 8)


def kernel(total, x_ref, spin_ref, hop_ref, bond_ref, u_ref, c_ref, G, F, recv, raw, xa, xp, relay, spin, en_ref, ebuf,
           lhi, llo, ec, whi, wlo, D, W, T, R, A2, z, x,
           share_sem, c_send, c_recv, e_send, e_recv,
           a_send, a_recv, own_sem, u_send, u_recv):
    pos, core = place()
    smp, par = lax.axis_index("smp"), lax.axis_index("par")
    n, kp = raw.shape
    nr = x_ref.shape[0]
    kc = kp // CHUNKS
    nb = n // B
    half = F.shape[2]
    plans = [plan(pos, core, q) for q in range(PORTIONS)]
    partner = device(pos, 1 - core)
    others = [(lax.rem(smp + d, 8), par) for d in range(1, 8)]
    peers = [partner] + [who for q in (0, 2, 4) for who in plans[q][1][0][1]] + others
    barrier = pltpu.get_barrier_semaphore()
    for who in peers:
        pl.semaphore_signal(barrier, inc=1, device_id=who, device_id_type=MESH)

    y, z_lo = lax.div(smp, 2), lax.rem(smp, 2)

    def seat(dy, dz):
        return lax.rem(y + dy + 4, 4) * 2 + (1 - z_lo if dz else z_lo)

    def sent(to, c):
        return pl.ds(pl.multiple_of(to * kp + c * kc, kc), kc)

    def landing(origin, row, rows, c):
        return raw.at[pl.ds(pl.multiple_of(origin * nr + row, rows), rows), c * kc : (c + 1) * kc]

    def straight(c):
        out = []
        for i, (dy, dz) in enumerate([(1, 0), (-1, 0), (1, 1), (-1, 1), (0, 1)]):
            to = seat(dy, dz)
            out.append(remote(x_ref.at[:, sent(to, c)], landing(smp, 0, nr, c), a_send.at[c, i], a_recv.at[c, i], (to, par)))
        return out

    def first_leg(c):
        out = []
        for d, way in enumerate((1, -1)):
            for dz in range(2):
                to = seat(2, dz)
                out.append(remote(
                    x_ref.at[d * (nr // 2) : (d + 1) * (nr // 2), sent(to, c)], relay.at[c, d, dz],
                    a_send.at[c, 5 + 2 * d + dz], a_recv.at[c, 5 + 2 * d + dz], (seat(way, 0), par)))
        return out

    def second_leg(c):
        out = []
        for d, way in enumerate((1, -1)):
            for dz in range(2):
                out.append(remote(
                    relay.at[c, d, dz], landing(seat(-way, 0), d * (nr // 2), nr // 2, c),
                    a_send.at[c, 9 + 2 * d + dz], a_recv.at[c, 9 + 2 * d + dz], (seat(way, dz), par)))
        return out

    def begin(c):
        legs, direct = first_leg(c), straight(c)
        for copy in legs + direct:
            copy.start()
        own = pltpu.make_async_copy(x_ref.at[:, sent(smp, c)], landing(smp, 0, nr, c), own_sem.at[c])
        own.start()
        return legs, direct, own

    def pass_on(c, legs):
        onward = second_leg(c)
        for leg, copy in zip(legs, onward):
            leg.wait_recv()
            copy.start()
        return onward

    scale = 1.0 / np.sqrt(np.float32(total))

    def energy():
        sites = spin_ref.shape[0]
        spin[...] = jnp.zeros_like(spin)
        spin[0:sites, :] = (2 * spin_ref[...] - 1).astype(jnp.float32)
        sigma = spin[...]
        field = lax.dot_general(bond_ref[...], sigma.astype(jnp.bfloat16), (NN, ((), ())), preferred_element_type=jnp.float32)
        row = jnp.sum(sigma * field, axis=0, keepdims=True) + hop_ref[...]
        en_ref[...] = jnp.broadcast_to(row, en_ref.shape)
        ebuf[pl.ds(smp, 1)] = en_ref[...][None]

    def center(c):
        cols = slice(c * kc, (c + 1) * kc)

        def add(i, acc):
            r = pl.ds(pl.multiple_of(i * 128, 128), 128)
            return acc + jnp.sum(raw[r, cols].astype(jnp.float32).reshape(16, 8, kc), axis=0)

        acc = lax.fori_loop(0, n // 128, add, jnp.zeros((8, kc), jnp.float32))
        mean = jnp.sum(acc, axis=0, keepdims=True) / total

        @pl.loop(0, n // 128)
        def _(i):
            r = pl.ds(pl.multiple_of(i * 128, 128), 128)
            xa[r, cols] = ((raw[r, cols].astype(jnp.float32) - mean) * scale).astype(jnp.bfloat16)

        share = remote(xa.at[:, cols], xp.at[:, cols], share_sem.at[c, 0], share_sem.at[c, 1], partner)
        share.start()
        return share

    starts = [nb * k - k * (k - 1) // 2 for k in range(1, nb)]

    def tiles(src, c, first):
        @pl.loop(0, 2 * (nb + 1))
        def _(it):
            a_local, j = lax.rem(it, 2), lax.div(it, 2)
            t = PACK * j + 2 * core + a_local
            k = sum(jnp.where(t >= start, 1, 0) for start in starts)
            i = t - (nb * k - lax.div(k * (k - 1), 2)) + k
            rows = src[block(i), c * kc : (c + 1) * kc]
            cols = src[block(k), c * kc : (c + 1) * kc]
            got = lax.dot_general(rows, cols, (NT, ((), ())), preferred_element_type=jnp.float32)
            at = (lax.div(j, 3), 2 * lax.rem(j, 3), pl.multiple_of(a_local * B, B))
            put(F, at, got if first else get(F, at) + got)

    energy()
    pl.semaphore_wait(barrier, len(peers))
    shares, moved = [], []
    spread = [remote(en_ref, ebuf.at[smp], e_send.at[d], e_recv.at[d], others[d]) for d in range(7)]
    flight = begin(0)
    for c in range(CHUNKS):
        legs, direct, own = flight
        onward = pass_on(c, legs)
        if c + 1 < CHUNKS:
            flight = begin(c + 1)
        else:
            for copy in spread:
                copy.start()
        for copy in direct + onward:
            copy.wait_recv()
        own.wait()
        moved += legs + direct + onward
        shares.append(center(c))
        tiles(xa, c, c == 0)
        shares[c].wait_recv()
        tiles(xp, c, False)
    portions = range(PORTIONS)
    base = []
    for q in portions:
        rows, at = half, jnp.int32(0)
        base.append([at])
        for _, bit in plans[q][0]:
            rows = rows // 2
            at = at + bit * rows
            base[q].append(at)
        for i, _ in plans[q][1]:
            rows = rows // 4
            at = at + i * rows
            base[q].append(at)
    size = [half, half // 2, half // 4, half // 16, half // 64]
    offs = [0, size[1], size[1] + size[2], size[1] + size[2] + 3 * size[3]]

    def part(ref, q, row, rows):
        return ref.at[:, q, pl.ds(eight(row), rows), :]

    def accumulate(q, row, rows, held):
        at = (slice(None), q, pl.ds(eight(row), rows), slice(None))
        F[at] += recv[:, q, pl.ds(eight(held), rows), :]

    sem = iter(range(10**6))
    pending = []

    def go(src, dst, who):
        i = next(sem)
        copy = remote(src, dst, c_send.at[i], c_recv.at[i], who)
        copy.start()
        pending.append(copy)
        return copy

    def halve(q, t):
        who, bit = plans[q][0][t]
        row = base[q][t] + (1 - bit) * size[t + 1]
        return go(part(F, q, row, size[t + 1]), part(recv, q, offs[t], size[t + 1]), who)

    def cut(q, stage):
        i, whos = plans[q][1][stage]
        rows = size[stage + 3]
        out = []
        for d, who in enumerate(whos):
            row = base[q][stage + 2] + lax.rem(i + d + 1, 4) * rows
            out.append(go(part(F, q, row, rows), part(recv, q, offs[stage + 2] + d * rows, rows), who))
        return out

    one = [halve(q, 0) for q in portions]
    two, three, four = [], [], []
    for q in portions:
        one[q].wait_recv()
        bit, rows = plans[q][0][1][1], size[2]
        accumulate(q, base[q][1] + (1 - bit) * rows, rows, offs[0] + (1 - bit) * rows)
        two.append(halve(q, 1))
        accumulate(q, base[q][2], rows, offs[0] + bit * rows)
    for q in portions:
        two[q].wait_recv()
        accumulate(q, base[q][2], size[2], offs[1])
        three.append(cut(q, 0))
    for q in portions:
        for d, copy in enumerate(three[q]):
            copy.wait_recv()
            accumulate(q, base[q][3], size[3], offs[2] + d * size[3])
        four.append(cut(q, 1))
    for q in portions:
        for d, copy in enumerate(four[q]):
            copy.wait_recv()
            accumulate(q, base[q][4], size[4], offs[3] + d * size[4])
        at = pl.ds(eight(core * half + base[q][4]), size[4])
        G[:, q, at, :] = F[:, q, pl.ds(eight(base[q][4]), size[4]), :]

    early, late = slice(0, 1), slice(1, 3)

    def region(q, some, row, rows):
        return G.at[some, q, pl.ds(eight(core * half + row), rows), :]

    def spread_out(q, some, stage):
        here = region(q, some, base[q][stage + 3], size[stage + 3])
        return [go(here, here, who) for who in plans[q][1][stage][1]]

    def double(q, some, t):
        here = region(q, some, base[q][t + 1], size[t + 1])
        return go(here, here, plans[q][0][t][0])

    def across(some):
        here = G.at[some, :, pl.ds(pl.multiple_of(core * half, half), half), :]
        return go(here, here, partner)

    def arrive(copies):
        for copy in copies:
            copy.wait_recv()

    def stage(name, some):
        return {
            "five": lambda q: spread_out(q, some, 1),
            "six": lambda q: spread_out(q, some, 0),
            "seven": lambda q: [double(q, some, 1)],
            "eight": lambda q: [double(q, some, 0)],
        }[name]

    def follow(before, name, some):
        out = []
        for q in portions:
            if before is not None:
                arrive(before[q])
            out.append(stage(name, some)(q))
        return out

    e5 = follow(None, "five", early)
    l5 = follow(None, "five", late)
    e6 = follow(e5, "six", early)
    e7 = follow(e6, "seven", early)
    l6 = follow(l5, "six", late)
    e8 = follow(e7, "eight", early)
    l7 = follow(l6, "seven", late)
    for q in portions:
        arrive(e8[q])
    e9 = across(early)

    for copy in spread:
        copy.wait()
    every = [ebuf[s, 0:1, :] for s in range(8)]
    mean = sum(jnp.sum(row, axis=1, keepdims=True) for row in every) / total
    ec[...] = jnp.zeros_like(ec)
    for s in range(8):
        ec[0:1, s * nr : (s + 1) * nr] = (every[s] - mean) * scale
    e9.wait_recv()
    flying = {}

    def hook_one():
        flying["l8"] = follow(l7, "eight", late)

    def hook_two():
        for q in portions:
            arrive(flying["l8"][q])
        flying["l9"] = across(late)

    def hook_three():
        flying["l9"].wait_recv()
        for copy in pending + shares + moved:
            copy.wait_send()

    solve(n, x, G, lhi, llo, ec, whi, wlo, D, W, T, R, A2, z, [lambda: None, hook_one, hook_two, hook_three])

    hi, lo = split(x[...])
    d = lambda a: lax.dot_general(a, xa[...], (NN, ((), ())), preferred_element_type=jnp.float32)
    u_ref[pl.ds(smp, 1)] = (d(hi) + d(lo))[0:8][None]
    here = u_ref.at[smp]
    final = [remote(here, here, u_send.at[i], u_recv.at[i], others[i]) for i in range(7)]
    for copy in final:
        copy.start()
    c_ref[...] = x[0:8, pl.ds(pl.multiple_of(smp * nr, nr), nr)]
    for copy in final:
        copy.wait()


SIDE = 10


def bonds(size):
    out = np.zeros((size, size), np.float32)
    for r in range(SIDE):
        for c in range(SIDE):
            for dr, dc, weight in ((0, 1, 0.25), (1, 0, 0.25), (1, 1, 0.125), (1, -1, 0.125)):
                out[r * SIDE + c, (r + dr) % SIDE * SIDE + (c + dc) % SIDE] += weight
    return out


def body(log_derivs, spins, hop_energy):
    nr = log_derivs.shape[0]
    n, kp = nr * 8, log_derivs.shape[1] // 8
    nb = n // B
    vm = pl.BlockSpec(memory_space=pltpu.VMEM)
    dma = pltpu.SemaphoreType.DMA
    f32, bf16 = jnp.float32, jnp.bfloat16
    u, coeffs = pl.pallas_call(
        functools.partial(kernel, n),
        out_shape=[jax.ShapeDtypeStruct((8, 8, kp), f32), jax.ShapeDtypeStruct((8, nr), f32)],
        in_specs=[pl.BlockSpec(memory_space=pl.ANY), vm, vm, vm],
        out_specs=[vm, vm],
        scratch_shapes=[
            pltpu.VMEM((3, PORTIONS, n // 2 + B, H), f32),
            pltpu.VMEM((3, PORTIONS, n // 4, H), f32),
            pltpu.VMEM((3, PORTIONS, n // 4, H), f32),
            pltpu.VMEM((n, kp), bf16),
            pltpu.VMEM((n, kp), bf16),
            pltpu.VMEM((n, kp), bf16),
            pltpu.VMEM((CHUNKS, 2, 2, nr // 2, kp // CHUNKS), bf16),
            pltpu.VMEM((H, nr), f32),
            pltpu.VMEM((8, nr), f32),
            pltpu.VMEM((8, 8, nr), f32),
            pltpu.VMEM((n, n), bf16),
            pltpu.VMEM((n, n), bf16),
            pltpu.VMEM((16, n), f32),
            pltpu.VMEM((nb, B, B), bf16),
            pltpu.VMEM((nb, B, B), bf16),
            pltpu.VMEM((H, H), f32),
            pltpu.VMEM((2, H, H), f32),
            pltpu.VMEM((128, H), f32),
            pltpu.VMEM((16, H), f32),
            pltpu.VMEM((128, H), f32),
            pltpu.VMEM((16, n), f32),
            pltpu.VMEM((16, n), f32),
            dma((CHUNKS, 2)), dma((150,)), dma((150,)), dma((7,)), dma((7,)),
            dma((CHUNKS, 13)), dma((CHUNKS, 13)), dma((CHUNKS,)), dma((7,)), dma((7,)),
        ],
        compiler_params=pltpu.CompilerParams(
            vmem_limit_bytes=58 * 2**20, collective_id=1, has_side_effects=True
        ),
    )(log_derivs, spins.T, hop_energy[None], jnp.asarray(bonds(H), bf16))
    return u[:, 0, :].reshape(-1), coeffs[0]


def solution(mesh):
    placed = (P("smp", "par"), P("smp", None), P("smp"))
    return jax.shard_map(
        body, mesh=mesh, in_specs=placed, out_specs=(P("par"), P("smp")), check_vma=False
    )
```

```python
import functools
import jax, jax.numpy as jnp
import numpy as np
from jax import lax
from jax.experimental import pallas as pl
from jax.experimental.pallas import tpu as pltpu
from jax.sharding import PartitionSpec as P

B = 256
H = 128
NT = ((1,), (1,))
NN = ((1,), (0,))


def split(x):
    hi = x.astype(jnp.bfloat16)
    return hi, (x - hi.astype(jnp.float32)).astype(jnp.bfloat16)


def dot3(ah, al, bh, bl, dims):
    d = lambda a, b: lax.dot_general(a, b, (dims, ((), ())), preferred_element_type=jnp.float32)
    return d(ah, bh) + (d(ah, bl) + d(al, bh))


def thin(x, bh, bl, dims):
    xh, xl = split(x)
    d = lambda a, b: lax.dot_general(a, b, (dims, ((), ())), preferred_element_type=jnp.float32)
    both = d(jnp.concatenate([xh, xl], axis=0), bh)
    return both[0:16] + (both[16:32] + d(xh, bl))


def splat(x):
    return jnp.broadcast_to(x, (8, H))


def factor_inverse(groups, T, R, A2, beside):
    lane = lax.broadcasted_iota(jnp.int32, (8, H), 1)
    sub = lax.broadcasted_iota(jnp.int32, (8, H), 0)
    out = []
    corner = [splat(groups[0][:, j : j + 1]) for j in range(8)]
    for p in range(16):
        if beside is not None:
            beside(p)
        lo, slot = 8 * p, p % 2
        pivots, at = groups[p], 64 * slot
        for j in range(8):
            T[at + 8 * j : at + 8 * j + 8, :] = corner[j]
        inside = (lane >= lo) & (lane < lo + 8)
        R[8 * slot : 8 * slot + 8, :] = jnp.where(inside, (lane - lo == sub).astype(jnp.float32), pivots)
        e = {}
        for j in range(8):
            for i in range(j, 8):
                e[i, j] = splat(T[at + 8 * j + i : at + 8 * j + i + 1, :])
        y = [splat(R[8 * slot + i : 8 * slot + i + 1, :]) for i in range(8)]
        last = p == 15
        if not last:
            near = groups[p + 1]
            a = [splat(near[:, lo + j : lo + j + 1]) for j in range(8)]
            corner = [splat(near[:, lo + 8 + j : lo + 9 + j]) for j in range(8)]
            near = jnp.where(inside, 0.0, near)
        m, r, u = {}, [], None
        for k in range(8):
            rk = pl.reciprocal(e[k, k], approx=True)
            r.append(rk)
            for i in range(k + 1, 8):
                m[i, k] = e[i, k] * rk
            for i in range(k + 1, 8):
                for q in range(k + 1, i + 1):
                    if i == q == k + 1:
                        e[i, q] = e[i, q] - (e[i, k] * e[i, k]) * rk
                    else:
                        e[i, q] = e[i, q] - m[i, k] * e[q, k]
            for i in range(k + 1, 8):
                y[i] = y[i] - m[i, k] * y[k]
            row = y[k] * lax.rsqrt(e[k, k])
            u = row if k == 0 else jnp.where(sub == k, row, u)
            if not last:
                for i in range(k + 1, 8):
                    a[i] = a[i] - m[i, k] * a[k]
                scaled = a[k] * rk
                A2[at + 8 * k : at + 8 * k + 8, :] = scaled
                near = near - scaled * y[k]
                for j in range(8):
                    corner[j] = corner[j] - a[k] * splat(A2[at + 8 * k + j : at + 8 * k + j + 1, :])
        out.append(u)
        if last:
            break
        groups[p + 1] = near
        v = [None] * 8
        for j in range(7, -1, -1):
            t = r[j] * y[j]
            for k in range(7, j, -1):
                t = t - m[k, j] * v[k]
            v[j] = t
        for g in range(p + 2, 16):
            old = groups[g]
            t = [splat(old[:, lo + j : lo + j + 1]) * v[j] for j in range(8)]
            t = ((t[0] + t[1]) + (t[2] + t[3])) + ((t[4] + t[5]) + (t[6] + t[7]))
            groups[g] = jnp.where(inside, 0.0, old) - t
    return [jnp.where(lane <= sub + 8 * g, out[g], 0.0) for g in range(16)]


def known(*xs):
    return all(isinstance(x, int) for x in xs)


def div(a, b):
    return a // b if known(a, b) else lax.div(jnp.int32(a), jnp.int32(b))


def rem(a, b):
    return a % b if known(a, b) else lax.rem(jnp.int32(a), jnp.int32(b))


def least(a, b):
    return min(a, b) if known(a, b) else jnp.minimum(a, b)


def choose(c, a, b):
    return (a if c else b) if isinstance(c, bool) else jnp.where(c, a, b)


def multiple(x, m):
    return x if known(x) else pl.multiple_of(x, m)


def slot(nb, i, k):
    return nb * k - div(k * (k - 1), 2) + i - k


def tile(nb, i, k):
    t = slot(nb, i, k)
    a, j = rem(t, PACK), div(t, PACK)
    return div(j, 3), 2 * rem(j, 3), multiple(a * B, B)


def get(G, at):
    s, q, r = at
    return jnp.concatenate([G[s, q, pl.ds(r, B), :], G[s, q + 1, pl.ds(r, B), :]], axis=1)


def put(G, at, value):
    s, q, r = at
    G[s, q, pl.ds(r, B), :] = value[:, 0:H]
    G[s, q + 1, pl.ds(r, B), :] = value[:, H:B]


def sub(G, at, value):
    s, q, r = at
    G[s, q, pl.ds(r, B), :] -= value[:, 0:H]
    G[s, q + 1, pl.ds(r, B), :] -= value[:, H:B]


def block(i):
    return pl.ds(multiple(i * B, B), B)


TRIANGLES = 6
PACK = 4


def solve(n, x_ref, G, lhi, llo, ec, whi, wlo, D, W, T, R, A2, z, hooks):
    nb = n // B
    diag = lax.broadcasted_iota(jnp.int32, (H, H), 0) == lax.broadcasted_iota(jnp.int32, (H, H), 1)
    damp = jnp.where(diag, jnp.float32(0.2), jnp.float32(0.0))

    def span(k):
        return slice(k * B, k * B + B) if isinstance(k, int) else block(k)

    def triangle(k, i, live):
        ch, cl = split(get(G, tile(nb, i, k)))
        th, tl = split(dot3(ch, cl, whi[k], wlo[k], NT))
        lhi[block(i), span(k)], llo[block(i), span(k)] = th, tl
        ec[:, block(i)] -= thin(z[:, span(k)], th, tl, NT) * live
        return th, tl

    def factor(k, h, slots):
        def beside(p):
            if h == 0 and p < TRIANGLES:
                triangle(k - 1, least(k + 1 + p, nb - 1), choose(k + 1 + p < nb, 1.0, 0.0))
                return
            if h == 0 and (p - TRIANGLES) % 2 != 0 or h == 1 and p >= 11:
                return
            s = (p - TRIANGLES) // 2 if h == 0 else 5 + p
            live = s < (k + 1) * (nb - 1 - k)
            i = least(k + 1 + div(s, k + 1), nb - 1)
            u = rem(s, k + 1)
            own = u == k
            column = choose(own, k, least(k + 1, nb - 1))
            j = choose(own, k - 1, u)
            at = tile(nb, i, column)
            at = (at[0], at[1], multiple(choose(live, at[2], n // 2), B))
            sub(G, at, dot3(
                lhi[block(i), block(j)], llo[block(i), block(j)],
                lhi[block(column), block(j)], llo[block(column), block(j)], NT))

        got = factor_inverse([D[8 * g : 8 * g + 8, :] for g in range(16)], T, R, A2, beside if slots else None)
        for g in range(16):
            W[h, 8 * g : 8 * g + 8, :] = got[g]

    def chain(k, h):
        if isinstance(k, int):
            factor(k, h, k > 0)
            return

        @pl.when(k < nb - 1)
        def _():
            factor(k, h, True)

        @pl.when(k == nb - 1)
        def _():
            factor(k, h, False)

    def at_place(k, place):
        if known(k) and (k, place) in hooks:
            hooks[k, place]()

    def panel(k):
        home = tile(nb, k, k)
        if not (known(k) and k == 0):
            th, tl = triangle(k - 1, k, 1.0)
            sub(G, home, dot3(th, tl, th, tl, NT))

        at_place(k, 0)
        hs, hq, hr = home
        top, low = pl.ds(hr, H), pl.ds(multiple(hr + H, H), H)
        D[...] = G[hs, hq, top, :] + damp
        chain(k, 0)
        at_place(k, 1)
        w1h, w1l = split(W[0])
        ah, al = split(G[hs, hq, low, :])
        lh, ll = split(dot3(ah, al, w1h, w1l, NT))
        D[...] = G[hs, hq + 1, low, :] + damp - dot3(lh, ll, lh, ll, NT)
        th, tl = split(dot3(lh, ll, w1h, w1l, NN))
        whi[k, 0:H, 0:H], wlo[k, 0:H, 0:H] = w1h, w1l
        whi[k, 0:H, H:B] = jnp.zeros((H, H), jnp.bfloat16)
        wlo[k, 0:H, H:B] = jnp.zeros((H, H), jnp.bfloat16)
        chain(k, 1)
        w2h, w2l = split(W[1])
        whi[k, H:B, H:B], wlo[k, H:B, H:B] = w2h, w2l
        whi[k, H:B, 0:H], wlo[k, H:B, 0:H] = split(-dot3(w2h, w2l, th, tl, NN))
        z[:, span(k)] = thin(ec[:, span(k)], whi[k], wlo[k], NT)
        at_place(k, 2)

    panel(0)
    panel(1)

    @pl.loop(2, nb)
    def _(k):
        panel(k)

    for kk in range(nb - 1, -1, -1):
        cols = slice(kk * B, kk * B + B)
        x = thin(z[:, cols], whi[kk], wlo[kk], NN)
        x_ref[:, cols] = x
        if kk > 0:
            z[:, : kk * B] -= thin(x, lhi[cols, : kk * B], llo[cols, : kk * B], NN)


MESH = pl.DeviceIdType.MESH
PORTIONS = 6
CHUNKS = 2


def place():
    smp, par = lax.axis_index("smp"), lax.axis_index("par")
    y, z_lo = lax.div(smp, 2), lax.rem(smp, 2)
    x, z_hi, core = lax.div(par, 4), lax.rem(lax.div(par, 2), 2), lax.rem(par, 2)
    return (x, y, z_hi * 2 + z_lo), core


def device(pos, core):
    x, y, z = pos
    return (y * 2 + lax.rem(z, 2), x * 4 + lax.div(z, 2) * 2 + core)


def plan(pos, core, q):
    first = q // 2

    def at(axis, i):
        there = list(pos)
        there[axis] = i
        return device(there, core)

    i = pos[first]
    low, high = lax.rem(i, 2), lax.div(i, 2)
    near, far = at(first, i + 1 - 2 * low), at(first, 3 - i)
    if q % 2 == 0:
        halves = [(near, lax.rem(low + high, 2)), (far, high)]
    else:
        halves = [(far, high), (near, low)]
    cuts = []
    for stage in (1, 2):
        axis = (first + stage) % 3
        cuts.append((pos[axis], [at(axis, lax.rem(pos[axis] + d, 4)) for d in (1, 2, 3)]))
    return halves, cuts


def remote(src, dst, send, recv, who):
    return pltpu.make_async_remote_copy(
        src_ref=src, dst_ref=dst, send_sem=send, recv_sem=recv, device_id=who, device_id_type=MESH
    )


def eight(x):
    return pl.multiple_of(x, 8)


def kernel(total, x_ref, spin_ref, hop_ref, bond_ref, o_ref, c_ref, u_ref, G, F, recv, raw, xa, xp, relay, spin, en_ref, ebuf,
           lhi, llo, ec, whi, wlo, D, W, T, R, A2, z, x,
           share_sem, c_send, c_recv, e_send, e_recv,
           a_send, a_recv, own_sem, u_send, u_recv):
    pos, core = place()
    smp, par = lax.axis_index("smp"), lax.axis_index("par")
    n, kp = raw.shape
    nr = x_ref.shape[0]
    kc = kp // CHUNKS
    nb = n // B
    half = F.shape[2]
    plans = [plan(pos, core, q) for q in range(PORTIONS)]
    partner = device(pos, 1 - core)
    others = [(lax.rem(smp + d, 8), par) for d in range(1, 8)]
    peers = [partner] + [who for q in (0, 2, 4) for who in plans[q][1][0][1]] + others
    barrier = pltpu.get_barrier_semaphore()
    for who in peers:
        pl.semaphore_signal(barrier, inc=1, device_id=who, device_id_type=MESH)

    y, z_lo = lax.div(smp, 2), lax.rem(smp, 2)

    def seat(dy, dz):
        return lax.rem(y + dy + 4, 4) * 2 + (1 - z_lo if dz else z_lo)

    def sent(to, c):
        return pl.ds(pl.multiple_of(to * kp + c * kc, kc), kc)

    def landing(origin, row, rows, c):
        return raw.at[pl.ds(pl.multiple_of(origin * nr + row, rows), rows), c * kc : (c + 1) * kc]

    def straight(c):
        out = []
        for i, (dy, dz) in enumerate([(1, 0), (-1, 0), (1, 1), (-1, 1), (0, 1)]):
            to = seat(dy, dz)
            out.append(remote(x_ref.at[:, sent(to, c)], landing(smp, 0, nr, c), a_send.at[c, i], a_recv.at[c, i], (to, par)))
        return out

    def first_leg(c):
        out = []
        for d, way in enumerate((1, -1)):
            for dz in range(2):
                to = seat(2, dz)
                out.append(remote(
                    x_ref.at[d * (nr // 2) : (d + 1) * (nr // 2), sent(to, c)], relay.at[c, d, dz],
                    a_send.at[c, 5 + 2 * d + dz], a_recv.at[c, 5 + 2 * d + dz], (seat(way, 0), par)))
        return out

    def second_leg(c):
        out = []
        for d, way in enumerate((1, -1)):
            for dz in range(2):
                out.append(remote(
                    relay.at[c, d, dz], landing(seat(-way, 0), d * (nr // 2), nr // 2, c),
                    a_send.at[c, 9 + 2 * d + dz], a_recv.at[c, 9 + 2 * d + dz], (seat(way, dz), par)))
        return out

    def begin(c):
        legs, direct = first_leg(c), straight(c)
        for copy in legs + direct:
            copy.start()
        own = pltpu.make_async_copy(x_ref.at[:, sent(smp, c)], landing(smp, 0, nr, c), own_sem.at[c])
        own.start()
        return legs, direct, own

    def pass_on(c, legs):
        onward = second_leg(c)
        for leg, copy in zip(legs, onward):
            leg.wait_recv()
            copy.start()
        return onward

    scale = 1.0 / np.sqrt(np.float32(total))

    def energy():
        sites = spin_ref.shape[0]
        spin[...] = jnp.zeros_like(spin)
        spin[0:sites, :] = (2 * spin_ref[...] - 1).astype(jnp.float32)
        sigma = spin[...]
        field = lax.dot_general(bond_ref[...], sigma.astype(jnp.bfloat16), (NN, ((), ())), preferred_element_type=jnp.float32)
        row = jnp.sum(sigma * field, axis=0, keepdims=True) + hop_ref[...]
        en_ref[...] = jnp.broadcast_to(row, en_ref.shape)
        ebuf[pl.ds(smp, 1)] = en_ref[...][None]

    def center(c):
        cols = slice(c * kc, (c + 1) * kc)

        def add(i, acc):
            r = pl.ds(pl.multiple_of(i * 128, 128), 128)
            return acc + jnp.sum(raw[r, cols].astype(jnp.float32).reshape(16, 8, kc), axis=0)

        acc = lax.fori_loop(0, n // 128, add, jnp.zeros((8, kc), jnp.float32))
        mean = jnp.sum(acc, axis=0, keepdims=True) / total

        @pl.loop(0, n // 128)
        def _(i):
            r = pl.ds(pl.multiple_of(i * 128, 128), 128)
            xa[r, cols] = ((raw[r, cols].astype(jnp.float32) - mean) * scale).astype(jnp.bfloat16)

        share = remote(xa.at[:, cols], xp.at[:, cols], share_sem.at[c, 0], share_sem.at[c, 1], partner)
        share.start()
        return share

    starts = [nb * k - k * (k - 1) // 2 for k in range(1, nb)]

    def tiles(src, c, first):
        @pl.loop(0, 2 * (nb + 1))
        def _(it):
            a_local, j = lax.rem(it, 2), lax.div(it, 2)
            t = PACK * j + 2 * core + a_local
            k = sum(jnp.where(t >= start, 1, 0) for start in starts)
            i = t - (nb * k - lax.div(k * (k - 1), 2)) + k
            rows = src[block(i), c * kc : (c + 1) * kc]
            cols = src[block(k), c * kc : (c + 1) * kc]
            got = lax.dot_general(rows, cols, (NT, ((), ())), preferred_element_type=jnp.float32)
            at = (lax.div(j, 3), 2 * lax.rem(j, 3), pl.multiple_of(a_local * B, B))
            put(F, at, got if first else get(F, at) + got)

    energy()
    pl.semaphore_wait(barrier, len(peers))
    shares, moved = [], []
    spread = [remote(en_ref, ebuf.at[smp], e_send.at[d], e_recv.at[d], others[d]) for d in range(7)]
    flight = begin(0)
    for c in range(CHUNKS):
        legs, direct, own = flight
        onward = pass_on(c, legs)
        if c + 1 < CHUNKS:
            flight = begin(c + 1)
        else:
            for copy in spread:
                copy.start()
        for copy in direct + onward:
            copy.wait_recv()
        own.wait()
        moved += legs + direct + onward
        shares.append(center(c))
        tiles(xa, c, c == 0)
        shares[c].wait_recv()
        tiles(xp, c, False)
    portions = range(PORTIONS)
    base = []
    for q in portions:
        rows, at = half, jnp.int32(0)
        base.append([at])
        for _, bit in plans[q][0]:
            rows = rows // 2
            at = at + bit * rows
            base[q].append(at)
        for i, _ in plans[q][1]:
            rows = rows // 4
            at = at + i * rows
            base[q].append(at)
    size = [half, half // 2, half // 4, half // 16, half // 64]
    offs = [0, size[1], size[1] + size[2], size[1] + size[2] + 3 * size[3]]

    def part(ref, q, row, rows):
        return ref.at[:, q, pl.ds(eight(row), rows), :]

    def accumulate(q, row, rows, held):
        at = (slice(None), q, pl.ds(eight(row), rows), slice(None))
        F[at] += recv[:, q, pl.ds(eight(held), rows), :]

    sem = iter(range(10**6))
    pending = []

    def go(src, dst, who):
        i = next(sem)
        copy = remote(src, dst, c_send.at[i], c_recv.at[i], who)
        copy.start()
        pending.append(copy)
        return copy

    def halve(q, t):
        who, bit = plans[q][0][t]
        row = base[q][t] + (1 - bit) * size[t + 1]
        return go(part(F, q, row, size[t + 1]), part(recv, q, offs[t], size[t + 1]), who)

    def cut(q, stage):
        i, whos = plans[q][1][stage]
        rows = size[stage + 3]
        out = []
        for d, who in enumerate(whos):
            row = base[q][stage + 2] + lax.rem(i + d + 1, 4) * rows
            out.append(go(part(F, q, row, rows), part(recv, q, offs[stage + 2] + d * rows, rows), who))
        return out

    one = [halve(q, 0) for q in portions]
    two, three, four = [], [], []
    for q in portions:
        one[q].wait_recv()
        bit, rows = plans[q][0][1][1], size[2]
        accumulate(q, base[q][1] + (1 - bit) * rows, rows, offs[0] + (1 - bit) * rows)
        two.append(halve(q, 1))
        accumulate(q, base[q][2], rows, offs[0] + bit * rows)
    for q in portions:
        two[q].wait_recv()
        accumulate(q, base[q][2], size[2], offs[1])
        three.append(cut(q, 0))
    for q in portions:
        for d, copy in enumerate(three[q]):
            copy.wait_recv()
            accumulate(q, base[q][3], size[3], offs[2] + d * size[3])
        four.append(cut(q, 1))
    for q in portions:
        for d, copy in enumerate(four[q]):
            copy.wait_recv()
            accumulate(q, base[q][4], size[4], offs[3] + d * size[4])
        at = pl.ds(eight(core * half + base[q][4]), size[4])
        G[:, q, at, :] = F[:, q, pl.ds(eight(base[q][4]), size[4]), :]

    early, late = slice(0, 2), slice(2, 3)

    def region(q, some, row, rows):
        return G.at[some, q, pl.ds(eight(core * half + row), rows), :]

    def spread_out(q, some, stage):
        here = region(q, some, base[q][stage + 3], size[stage + 3])
        return [go(here, here, who) for who in plans[q][1][stage][1]]

    def double(q, some, t):
        here = region(q, some, base[q][t + 1], size[t + 1])
        return go(here, here, plans[q][0][t][0])

    def across(some):
        here = G.at[some, :, pl.ds(pl.multiple_of(core * half, half), half), :]
        return go(here, here, partner)

    def arrive(copies):
        for copy in copies:
            copy.wait_recv()

    def stage(name, some):
        return {
            "five": lambda q: spread_out(q, some, 1),
            "six": lambda q: spread_out(q, some, 0),
            "seven": lambda q: [double(q, some, 1)],
            "eight": lambda q: [double(q, some, 0)],
        }[name]

    def follow(before, name, some):
        out = []
        for q in portions:
            if before is not None:
                arrive(before[q])
            out.append(stage(name, some)(q))
        return out

    e5 = follow(None, "five", early)
    e6 = follow(e5, "six", early)
    e7 = follow(e6, "seven", early)
    e8 = follow(e7, "eight", early)
    own = len(pending)
    l5 = follow(None, "five", late)
    for q in portions:
        arrive(e8[q])
    e9, f9 = across(slice(0, 1)), across(slice(1, 2))
    early_sends = pending[:own] + pending[-2:]

    for copy in spread:
        copy.wait()
    every = [ebuf[s, 0:1, :] for s in range(8)]
    mean = sum(jnp.sum(row, axis=1, keepdims=True) for row in every) / total
    ec[...] = jnp.zeros_like(ec)
    for s in range(8):
        ec[0:1, s * nr : (s + 1) * nr] = (every[s] - mean) * scale
    e9.wait_recv()
    flying = {}

    def six():
        flying[6] = follow(l5, "six", late)

    def seven():
        flying[7] = follow(flying[6], "seven", late)

    def eight_():
        flying[8] = follow(flying[7], "eight", late)
        f9.wait_recv()
        for copy in early_sends + shares + moved:
            copy.wait_send()

    def nine():
        for q in portions:
            arrive(flying[8][q])
        flying[9] = across(late)

    def rest():
        flying[9].wait_recv()
        for copy in pending:
            if all(copy is not other for other in early_sends):
                copy.wait_send()

    hooks = {(0, 0): six, (0, 1): seven, (0, 2): eight_, (1, 1): nine, (1, 2): rest}
    solve(n, x, G, lhi, llo, ec, whi, wlo, D, W, T, R, A2, z, hooks)

    hi, lo = split(x[...])
    d = lambda a: lax.dot_general(a, xa[...], (NN, ((), ())), preferred_element_type=jnp.float32)
    u_ref[pl.ds(smp, 1)] = (d(hi) + d(lo))[0:8][None]
    here = u_ref.at[smp]
    final = [remote(here, here, u_send.at[i], u_recv.at[i], others[i]) for i in range(7)]
    for copy in final:
        copy.start()
    c_ref[...] = x[0:1, pl.ds(pl.multiple_of(smp * nr, nr), nr)]
    for copy in final:
        copy.wait()
    for s in range(8):
        o_ref[0:1, s * kp : (s + 1) * kp] = u_ref[s, 0:1, :]


SIDE = 10


def bonds(size):
    out = np.zeros((size, size), np.float32)
    for r in range(SIDE):
        for c in range(SIDE):
            for dr, dc, weight in ((0, 1, 0.25), (1, 0, 0.25), (1, 1, 0.125), (1, -1, 0.125)):
                out[r * SIDE + c, (r + dr) % SIDE * SIDE + (c + dc) % SIDE] += weight
    return out


def body(log_derivs, spins, hop_energy):
    nr = log_derivs.shape[0]
    n, kp = nr * 8, log_derivs.shape[1] // 8
    nb = n // B
    vm = pl.BlockSpec(memory_space=pltpu.VMEM)
    dma = pltpu.SemaphoreType.DMA
    f32, bf16 = jnp.float32, jnp.bfloat16
    u, coeffs = pl.pallas_call(
        functools.partial(kernel, n),
        out_shape=[jax.ShapeDtypeStruct((1, 8 * kp), f32), jax.ShapeDtypeStruct((1, nr), f32)],
        in_specs=[pl.BlockSpec(memory_space=pl.ANY), vm, vm, vm],
        out_specs=[vm, vm],
        scratch_shapes=[
            pltpu.VMEM((8, 8, kp), f32),
            pltpu.VMEM((3, PORTIONS, n // 2 + B, H), f32),
            pltpu.VMEM((3, PORTIONS, n // 4, H), f32),
            pltpu.VMEM((3, PORTIONS, n // 4, H), f32),
            pltpu.VMEM((n, kp), bf16),
            pltpu.VMEM((n, kp), bf16),
            pltpu.VMEM((n, kp), bf16),
            pltpu.VMEM((CHUNKS, 2, 2, nr // 2, kp // CHUNKS), bf16),
            pltpu.VMEM((H, nr), f32),
            pltpu.VMEM((8, nr), f32),
            pltpu.VMEM((8, 8, nr), f32),
            pltpu.VMEM((n, n), bf16),
            pltpu.VMEM((n, n), bf16),
            pltpu.VMEM((16, n), f32),
            pltpu.VMEM((nb, B, B), bf16),
            pltpu.VMEM((nb, B, B), bf16),
            pltpu.VMEM((H, H), f32),
            pltpu.VMEM((2, H, H), f32),
            pltpu.VMEM((128, H), f32),
            pltpu.VMEM((16, H), f32),
            pltpu.VMEM((128, H), f32),
            pltpu.VMEM((16, n), f32),
            pltpu.VMEM((16, n), f32),
            dma((CHUNKS, 2)), dma((150,)), dma((150,)), dma((7,)), dma((7,)),
            dma((CHUNKS, 13)), dma((CHUNKS, 13)), dma((CHUNKS,)), dma((7,)), dma((7,)),
        ],
        compiler_params=pltpu.CompilerParams(
            vmem_limit_bytes=58 * 2**20, collective_id=1, has_side_effects=True
        ),
    )(log_derivs, spins.T, hop_energy[None], jnp.asarray(bonds(H), bf16))
    return u.reshape(-1), coeffs.reshape(-1)


def solution(mesh):
    placed = (P("smp", "par"), P("smp", None), P("smp"))
    return jax.shard_map(
        body, mesh=mesh, in_specs=placed, out_specs=(P("par"), P("smp")), check_vma=False
    )
```

```python
import functools
import jax, jax.numpy as jnp
import numpy as np
from jax import lax
from jax.experimental import pallas as pl
from jax.experimental.pallas import tpu as pltpu
from jax.sharding import PartitionSpec as P

B = 256
H = 128
NT = ((1,), (1,))
NN = ((1,), (0,))


def split(x):
    hi = x.astype(jnp.bfloat16)
    return hi, (x - hi.astype(jnp.float32)).astype(jnp.bfloat16)


def dot3(ah, al, bh, bl, dims):
    d = lambda a, b: lax.dot_general(a, b, (dims, ((), ())), preferred_element_type=jnp.float32)
    return d(ah, bh) + (d(ah, bl) + d(al, bh))


def thin(x, bh, bl, dims):
    xh, xl = split(x)
    d = lambda a, b: lax.dot_general(a, b, (dims, ((), ())), preferred_element_type=jnp.float32)
    both = d(jnp.concatenate([xh, xl], axis=0), bh)
    return both[0:16] + (both[16:32] + d(xh, bl))


def splat(x):
    return jnp.broadcast_to(x, (8, H))


def factor_inverse(groups, T, R, A2, beside):
    lane = lax.broadcasted_iota(jnp.int32, (8, H), 1)
    sub = lax.broadcasted_iota(jnp.int32, (8, H), 0)
    out = []
    corner = [splat(groups[0][:, j : j + 1]) for j in range(8)]
    for p in range(16):
        if beside is not None:
            beside(p)
        lo, slot = 8 * p, p % 2
        pivots, at = groups[p], 64 * slot
        for j in range(8):
            T[at + 8 * j : at + 8 * j + 8, :] = corner[j]
        inside = (lane >= lo) & (lane < lo + 8)
        R[8 * slot : 8 * slot + 8, :] = jnp.where(inside, (lane - lo == sub).astype(jnp.float32), pivots)
        e = {}
        for j in range(8):
            for i in range(j, 8):
                e[i, j] = splat(T[at + 8 * j + i : at + 8 * j + i + 1, :])
        y = [splat(R[8 * slot + i : 8 * slot + i + 1, :]) for i in range(8)]
        last = p == 15
        if not last:
            near = groups[p + 1]
            a = [splat(near[:, lo + j : lo + j + 1]) for j in range(8)]
            corner = [splat(near[:, lo + 8 + j : lo + 9 + j]) for j in range(8)]
            near = jnp.where(inside, 0.0, near)
        m, r, u = {}, [], None
        for k in range(8):
            rk = pl.reciprocal(e[k, k], approx=True)
            r.append(rk)
            for i in range(k + 1, 8):
                m[i, k] = e[i, k] * rk
            for i in range(k + 1, 8):
                for q in range(k + 1, i + 1):
                    if i == q == k + 1:
                        e[i, q] = e[i, q] - (e[i, k] * e[i, k]) * rk
                    else:
                        e[i, q] = e[i, q] - m[i, k] * e[q, k]
            for i in range(k + 1, 8):
                y[i] = y[i] - m[i, k] * y[k]
            row = y[k] * lax.rsqrt(e[k, k])
            u = row if k == 0 else jnp.where(sub == k, row, u)
            if not last:
                for i in range(k + 1, 8):
                    a[i] = a[i] - m[i, k] * a[k]
                scaled = a[k] * rk
                A2[at + 8 * k : at + 8 * k + 8, :] = scaled
                near = near - scaled * y[k]
                for j in range(8):
                    corner[j] = corner[j] - a[k] * splat(A2[at + 8 * k + j : at + 8 * k + j + 1, :])
        out.append(u)
        if last:
            break
        groups[p + 1] = near
        v = [None] * 8
        for j in range(7, -1, -1):
            t = r[j] * y[j]
            for k in range(7, j, -1):
                t = t - m[k, j] * v[k]
            v[j] = t
        for g in range(p + 2, 16):
            old = groups[g]
            t = [splat(old[:, lo + j : lo + j + 1]) * v[j] for j in range(8)]
            t = ((t[0] + t[1]) + (t[2] + t[3])) + ((t[4] + t[5]) + (t[6] + t[7]))
            groups[g] = jnp.where(inside, 0.0, old) - t
    return [jnp.where(lane <= sub + 8 * g, out[g], 0.0) for g in range(16)]


def known(*xs):
    return all(isinstance(x, int) for x in xs)


def div(a, b):
    return a // b if known(a, b) else lax.div(jnp.int32(a), jnp.int32(b))


def rem(a, b):
    return a % b if known(a, b) else lax.rem(jnp.int32(a), jnp.int32(b))


def least(a, b):
    return min(a, b) if known(a, b) else jnp.minimum(a, b)


def choose(c, a, b):
    return (a if c else b) if isinstance(c, bool) else jnp.where(c, a, b)


def multiple(x, m):
    return x if known(x) else pl.multiple_of(x, m)


def slot(nb, i, k):
    return nb * k - div(k * (k - 1), 2) + i - k


def tile(nb, i, k):
    t = slot(nb, i, k)
    a, j = rem(t, PACK), div(t, PACK)
    return div(j, 3), 2 * rem(j, 3), multiple(a * B, B)


def get(G, at):
    s, q, r = at
    return jnp.concatenate([G[s, q, pl.ds(r, B), :], G[s, q + 1, pl.ds(r, B), :]], axis=1)


def put(G, at, value):
    s, q, r = at
    G[s, q, pl.ds(r, B), :] = value[:, 0:H]
    G[s, q + 1, pl.ds(r, B), :] = value[:, H:B]


def sub(G, at, value):
    s, q, r = at
    G[s, q, pl.ds(r, B), :] -= value[:, 0:H]
    G[s, q + 1, pl.ds(r, B), :] -= value[:, H:B]


def block(i):
    return pl.ds(multiple(i * B, B), B)


TRIANGLES = 6
PACK = 4


def solve(n, x_ref, G, lhi, llo, ec, whi, wlo, D, W, T, R, A2, z, hooks):
    nb = n // B
    diag = lax.broadcasted_iota(jnp.int32, (H, H), 0) == lax.broadcasted_iota(jnp.int32, (H, H), 1)
    damp = jnp.where(diag, jnp.float32(0.2), jnp.float32(0.0))

    def span(k):
        return slice(k * B, k * B + B) if isinstance(k, int) else block(k)

    def triangle(k, i, live):
        ch, cl = split(get(G, tile(nb, i, k)))
        th, tl = split(dot3(ch, cl, whi[k], wlo[k], NT))
        lhi[block(i), span(k)], llo[block(i), span(k)] = th, tl
        ec[:, block(i)] -= thin(z[:, span(k)], th, tl, NT) * live
        return th, tl

    def factor(k, h, slots):
        def beside(p):
            if h == 0 and p < TRIANGLES:
                triangle(k - 1, least(k + 1 + p, nb - 1), choose(k + 1 + p < nb, 1.0, 0.0))
                return
            if h == 0 and (p - TRIANGLES) % 2 != 0 or h == 1 and p >= 11:
                return
            s = (p - TRIANGLES) // 2 if h == 0 else 5 + p
            live = s < (k + 1) * (nb - 1 - k)
            i = least(k + 1 + div(s, k + 1), nb - 1)
            u = rem(s, k + 1)
            own = u == k
            column = choose(own, k, least(k + 1, nb - 1))
            j = choose(own, k - 1, u)
            at = tile(nb, i, column)
            at = (at[0], at[1], multiple(choose(live, at[2], n // 2), B))
            sub(G, at, dot3(
                lhi[block(i), block(j)], llo[block(i), block(j)],
                lhi[block(column), block(j)], llo[block(column), block(j)], NT))

        got = factor_inverse([D[8 * g : 8 * g + 8, :] for g in range(16)], T, R, A2, beside if slots else None)
        for g in range(16):
            W[h, 8 * g : 8 * g + 8, :] = got[g]

    def chain(k, h):
        if isinstance(k, int):
            factor(k, h, k > 0)
            return

        @pl.when(k < nb - 1)
        def _():
            factor(k, h, True)

        @pl.when(k == nb - 1)
        def _():
            factor(k, h, False)

    def at_place(k, place):
        if known(k) and (k, place) in hooks:
            hooks[k, place]()

    def panel(k):
        home = tile(nb, k, k)
        if not (known(k) and k == 0):
            th, tl = triangle(k - 1, k, 1.0)
            sub(G, home, dot3(th, tl, th, tl, NT))

        at_place(k, 0)
        hs, hq, hr = home
        top, low = pl.ds(hr, H), pl.ds(multiple(hr + H, H), H)
        D[...] = G[hs, hq, top, :] + damp
        chain(k, 0)
        at_place(k, 1)
        w1h, w1l = split(W[0])
        ah, al = split(G[hs, hq, low, :])
        lh, ll = split(dot3(ah, al, w1h, w1l, NT))
        D[...] = G[hs, hq + 1, low, :] + damp - dot3(lh, ll, lh, ll, NT)
        th, tl = split(dot3(lh, ll, w1h, w1l, NN))
        whi[k, 0:H, 0:H], wlo[k, 0:H, 0:H] = w1h, w1l
        whi[k, 0:H, H:B] = jnp.zeros((H, H), jnp.bfloat16)
        wlo[k, 0:H, H:B] = jnp.zeros((H, H), jnp.bfloat16)
        chain(k, 1)
        w2h, w2l = split(W[1])
        whi[k, H:B, H:B], wlo[k, H:B, H:B] = w2h, w2l
        whi[k, H:B, 0:H], wlo[k, H:B, 0:H] = split(-dot3(w2h, w2l, th, tl, NN))
        z[:, span(k)] = thin(ec[:, span(k)], whi[k], wlo[k], NT)
        at_place(k, 2)

    panel(0)
    panel(1)

    @pl.loop(2, nb)
    def _(k):
        panel(k)

    for kk in range(nb - 1, -1, -1):
        cols = slice(kk * B, kk * B + B)
        x = thin(z[:, cols], whi[kk], wlo[kk], NN)
        x_ref[:, cols] = x
        if kk > 0:
            z[:, : kk * B] -= thin(x, lhi[cols, : kk * B], llo[cols, : kk * B], NN)


MESH = pl.DeviceIdType.MESH
PORTIONS = 6
CHUNKS = 2


def place():
    smp, par = lax.axis_index("smp"), lax.axis_index("par")
    y, z_lo = lax.div(smp, 2), lax.rem(smp, 2)
    x, z_hi, core = lax.div(par, 4), lax.rem(lax.div(par, 2), 2), lax.rem(par, 2)
    return (x, y, z_hi * 2 + z_lo), core


def device(pos, core):
    x, y, z = pos
    return (y * 2 + lax.rem(z, 2), x * 4 + lax.div(z, 2) * 2 + core)


def plan(pos, core, q):
    first = q // 2

    def at(axis, i):
        there = list(pos)
        there[axis] = i
        return device(there, core)

    i = pos[first]
    low, high = lax.rem(i, 2), lax.div(i, 2)
    near, far = at(first, i + 1 - 2 * low), at(first, 3 - i)
    if q % 2 == 0:
        halves = [(near, lax.rem(low + high, 2)), (far, high)]
    else:
        halves = [(far, high), (near, low)]
    cuts = []
    for stage in (1, 2):
        axis = (first + stage) % 3
        cuts.append((pos[axis], [at(axis, lax.rem(pos[axis] + d, 4)) for d in (1, 2, 3)]))
    return halves, cuts


def remote(src, dst, send, recv, who):
    return pltpu.make_async_remote_copy(
        src_ref=src, dst_ref=dst, send_sem=send, recv_sem=recv, device_id=who, device_id_type=MESH
    )


def eight(x):
    return pl.multiple_of(x, 8)


def kernel(total, x_ref, spin_ref, hop_ref, bond_ref, o_ref, c_ref, u_ref, G, F, recv, raw, xa, xp, relay, spin, en_ref, ebuf,
           lhi, llo, ec, whi, wlo, D, W, T, R, A2, z, x,
           share_sem, c_send, c_recv, e_send, e_recv,
           a_send, a_recv, own_sem, u_send, u_recv):
    pos, core = place()
    smp, par = lax.axis_index("smp"), lax.axis_index("par")
    n, kp = raw.shape
    nr = x_ref.shape[0]
    kc = kp // CHUNKS
    nb = n // B
    half = F.shape[2]
    plans = [plan(pos, core, q) for q in range(PORTIONS)]
    partner = device(pos, 1 - core)
    others = [(lax.rem(smp + d, 8), par) for d in range(1, 8)]
    peers = [partner] + [who for q in (0, 2, 4) for who in plans[q][1][0][1]] + others
    barrier = pltpu.get_barrier_semaphore()
    for who in peers:
        pl.semaphore_signal(barrier, inc=1, device_id=who, device_id_type=MESH)

    y, z_lo = lax.div(smp, 2), lax.rem(smp, 2)

    def seat(dy, dz):
        return lax.rem(y + dy + 4, 4) * 2 + (1 - z_lo if dz else z_lo)

    def sent(to, c):
        return pl.ds(pl.multiple_of(to * kp + c * kc, kc), kc)

    def landing(origin, row, rows, c):
        return raw.at[pl.ds(pl.multiple_of(origin * nr + row, rows), rows), c * kc : (c + 1) * kc]

    def straight(c):
        out = []
        for i, (dy, dz) in enumerate([(1, 0), (-1, 0), (1, 1), (-1, 1), (0, 1)]):
            to = seat(dy, dz)
            out.append(remote(x_ref.at[:, sent(to, c)], landing(smp, 0, nr, c), a_send.at[c, i], a_recv.at[c, i], (to, par)))
        return out

    def first_leg(c):
        out = []
        for d, way in enumerate((1, -1)):
            for dz in range(2):
                to = seat(2, dz)
                out.append(remote(
                    x_ref.at[d * (nr // 2) : (d + 1) * (nr // 2), sent(to, c)], relay.at[c, d, dz],
                    a_send.at[c, 5 + 2 * d + dz], a_recv.at[c, 5 + 2 * d + dz], (seat(way, 0), par)))
        return out

    def second_leg(c):
        out = []
        for d, way in enumerate((1, -1)):
            for dz in range(2):
                out.append(remote(
                    relay.at[c, d, dz], landing(seat(-way, 0), d * (nr // 2), nr // 2, c),
                    a_send.at[c, 9 + 2 * d + dz], a_recv.at[c, 9 + 2 * d + dz], (seat(way, dz), par)))
        return out

    def begin(c):
        legs, direct = first_leg(c), straight(c)
        for copy in legs + direct:
            copy.start()
        own = pltpu.make_async_copy(x_ref.at[:, sent(smp, c)], landing(smp, 0, nr, c), own_sem.at[c])
        own.start()
        return legs, direct, own

    def pass_on(c, legs):
        onward = second_leg(c)
        for leg, copy in zip(legs, onward):
            leg.wait_recv()
            copy.start()
        return onward

    scale = 1.0 / np.sqrt(np.float32(total))

    def energy():
        sites = spin_ref.shape[0]
        spin[...] = jnp.zeros_like(spin)
        spin[0:sites, :] = (2 * spin_ref[...] - 1).astype(jnp.float32)
        sigma = spin[...]
        field = lax.dot_general(bond_ref[...], sigma.astype(jnp.bfloat16), (NN, ((), ())), preferred_element_type=jnp.float32)
        row = jnp.sum(sigma * field, axis=0, keepdims=True) + hop_ref[...]
        en_ref[...] = jnp.broadcast_to(row, en_ref.shape)
        ebuf[pl.ds(smp, 1)] = en_ref[...][None]

    def center(c):
        cols = slice(c * kc, (c + 1) * kc)

        def add(i, acc):
            r = pl.ds(pl.multiple_of(i * 128, 128), 128)
            return acc + jnp.sum(raw[r, cols].astype(jnp.float32).reshape(16, 8, kc), axis=0)

        acc = lax.fori_loop(0, n // 128, add, jnp.zeros((8, kc), jnp.float32))
        mean = jnp.sum(acc, axis=0, keepdims=True) / total

        @pl.loop(0, n // 128)
        def _(i):
            r = pl.ds(pl.multiple_of(i * 128, 128), 128)
            xa[r, cols] = ((raw[r, cols].astype(jnp.float32) - mean) * scale).astype(jnp.bfloat16)

        share = remote(xa.at[:, cols], xp.at[:, cols], share_sem.at[c, 0], share_sem.at[c, 1], partner)
        share.start()
        return share

    starts = [nb * k - k * (k - 1) // 2 for k in range(1, nb)]

    def tiles(src, c, first):
        @pl.loop(0, 2 * (nb + 1))
        def _(it):
            a_local, j = lax.rem(it, 2), lax.div(it, 2)
            t = PACK * j + 2 * core + a_local
            k = sum(jnp.where(t >= start, 1, 0) for start in starts)
            i = t - (nb * k - lax.div(k * (k - 1), 2)) + k
            rows = src[block(i), c * kc : (c + 1) * kc]
            cols = src[block(k), c * kc : (c + 1) * kc]
            got = lax.dot_general(rows, cols, (NT, ((), ())), preferred_element_type=jnp.float32)
            at = (lax.div(j, 3), 2 * lax.rem(j, 3), pl.multiple_of(a_local * B, B))
            put(F, at, got if first else get(F, at) + got)

    energy()
    pl.semaphore_wait(barrier, len(peers))
    shares, moved = [], []
    spread = [remote(en_ref, ebuf.at[smp], e_send.at[d], e_recv.at[d], others[d]) for d in range(7)]
    legs, direct, own = begin(0)
    onward = pass_on(0, legs)
    for c in range(CHUNKS):
        if c + 1 < CHUNKS:
            later = begin(c + 1)
        else:
            for copy in spread:
                copy.start()
        for copy in direct + onward:
            copy.wait_recv()
        own.wait()
        moved += legs + direct + onward
        shares.append(center(c))
        if c + 1 < CHUNKS:
            legs, direct, own = later
            onward = pass_on(c + 1, legs)
        tiles(xa, c, c == 0)
        shares[c].wait_recv()
        tiles(xp, c, False)
    portions = range(PORTIONS)
    base = []
    for q in portions:
        rows, at = half, jnp.int32(0)
        base.append([at])
        for _, bit in plans[q][0]:
            rows = rows // 2
            at = at + bit * rows
            base[q].append(at)
        for i, _ in plans[q][1]:
            rows = rows // 4
            at = at + i * rows
            base[q].append(at)
    size = [half, half // 2, half // 4, half // 16, half // 64]
    offs = [0, size[1], size[1] + size[2], size[1] + size[2] + 3 * size[3]]

    def part(ref, q, row, rows):
        return ref.at[:, q, pl.ds(eight(row), rows), :]

    def accumulate(q, row, rows, held):
        at = (slice(None), q, pl.ds(eight(row), rows), slice(None))
        F[at] += recv[:, q, pl.ds(eight(held), rows), :]

    sem = iter(range(10**6))
    pending = []

    def go(src, dst, who):
        i = next(sem)
        copy = remote(src, dst, c_send.at[i], c_recv.at[i], who)
        copy.start()
        pending.append(copy)
        return copy

    def halve(q, t):
        who, bit = plans[q][0][t]
        row = base[q][t] + (1 - bit) * size[t + 1]
        return go(part(F, q, row, size[t + 1]), part(recv, q, offs[t], size[t + 1]), who)

    def cut(q, stage):
        i, whos = plans[q][1][stage]
        rows = size[stage + 3]
        out = []
        for d, who in enumerate(whos):
            row = base[q][stage + 2] + lax.rem(i + d + 1, 4) * rows
            out.append(go(part(F, q, row, rows), part(recv, q, offs[stage + 2] + d * rows, rows), who))
        return out

    one = [halve(q, 0) for q in portions]
    two, three, four = [], [], []
    for q in portions:
        one[q].wait_recv()
        bit, rows = plans[q][0][1][1], size[2]
        accumulate(q, base[q][1] + (1 - bit) * rows, rows, offs[0] + (1 - bit) * rows)
        two.append(halve(q, 1))
        accumulate(q, base[q][2], rows, offs[0] + bit * rows)
    for q in portions:
        two[q].wait_recv()
        accumulate(q, base[q][2], size[2], offs[1])
        three.append(cut(q, 0))
    for q in portions:
        for d, copy in enumerate(three[q]):
            copy.wait_recv()
            accumulate(q, base[q][3], size[3], offs[2] + d * size[3])
        four.append(cut(q, 1))
    for q in portions:
        for d, copy in enumerate(four[q]):
            copy.wait_recv()
            accumulate(q, base[q][4], size[4], offs[3] + d * size[4])
        at = pl.ds(eight(core * half + base[q][4]), size[4])
        G[:, q, at, :] = F[:, q, pl.ds(eight(base[q][4]), size[4]), :]

    early, late = slice(0, 2), slice(2, 3)

    def region(q, some, row, rows):
        return G.at[some, q, pl.ds(eight(core * half + row), rows), :]

    def spread_out(q, some, stage):
        here = region(q, some, base[q][stage + 3], size[stage + 3])
        return [go(here, here, who) for who in plans[q][1][stage][1]]

    def double(q, some, t):
        here = region(q, some, base[q][t + 1], size[t + 1])
        return go(here, here, plans[q][0][t][0])

    def across(some):
        here = G.at[some, :, pl.ds(pl.multiple_of(core * half, half), half), :]
        return go(here, here, partner)

    def arrive(copies):
        for copy in copies:
            copy.wait_recv()

    def stage(name, some):
        return {
            "five": lambda q: spread_out(q, some, 1),
            "six": lambda q: spread_out(q, some, 0),
            "seven": lambda q: [double(q, some, 1)],
            "eight": lambda q: [double(q, some, 0)],
        }[name]

    def follow(before, name, some):
        out = []
        for q in portions:
            if before is not None:
                arrive(before[q])
            out.append(stage(name, some)(q))
        return out

    e5 = follow(None, "five", early)
    e6 = follow(e5, "six", early)
    e7 = follow(e6, "seven", early)
    e8 = follow(e7, "eight", early)
    own = len(pending)
    l5 = follow(None, "five", late)
    for q in portions:
        arrive(e8[q])
    e9, f9 = across(slice(0, 1)), across(slice(1, 2))
    early_sends = pending[:own] + pending[-2:]

    for copy in spread:
        copy.wait()
    every = [ebuf[s, 0:1, :] for s in range(8)]
    mean = sum(jnp.sum(row, axis=1, keepdims=True) for row in every) / total
    ec[...] = jnp.zeros_like(ec)
    for s in range(8):
        ec[0:1, s * nr : (s + 1) * nr] = (every[s] - mean) * scale
    e9.wait_recv()
    flying = {}

    def six():
        flying[6] = follow(l5, "six", late)

    def seven():
        flying[7] = follow(flying[6], "seven", late)

    def eight_():
        flying[8] = follow(flying[7], "eight", late)
        f9.wait_recv()
        for copy in early_sends + shares + moved:
            copy.wait_send()

    def nine():
        for q in portions:
            arrive(flying[8][q])
        flying[9] = across(late)

    def rest():
        flying[9].wait_recv()
        for copy in pending:
            if all(copy is not other for other in early_sends):
                copy.wait_send()

    hooks = {(0, 0): six, (0, 1): seven, (0, 2): eight_, (1, 1): nine, (1, 2): rest}
    solve(n, x, G, lhi, llo, ec, whi, wlo, D, W, T, R, A2, z, hooks)

    hi, lo = split(x[...])
    d = lambda a: lax.dot_general(a, xa[...], (NN, ((), ())), preferred_element_type=jnp.float32)
    u_ref[pl.ds(smp, 1)] = (d(hi) + d(lo))[0:8][None]
    here = u_ref.at[smp]
    final = [remote(here, here, u_send.at[i], u_recv.at[i], others[i]) for i in range(7)]
    for copy in final:
        copy.start()
    c_ref[...] = x[0:1, pl.ds(pl.multiple_of(smp * nr, nr), nr)]
    for copy in final:
        copy.wait()
    for s in range(8):
        o_ref[0:1, s * kp : (s + 1) * kp] = u_ref[s, 0:1, :]


SIDE = 10


def bonds(size):
    out = np.zeros((size, size), np.float32)
    for r in range(SIDE):
        for c in range(SIDE):
            for dr, dc, weight in ((0, 1, 0.25), (1, 0, 0.25), (1, 1, 0.125), (1, -1, 0.125)):
                out[r * SIDE + c, (r + dr) % SIDE * SIDE + (c + dc) % SIDE] += weight
    return out


def body(log_derivs, spins, hop_energy):
    nr = log_derivs.shape[0]
    n, kp = nr * 8, log_derivs.shape[1] // 8
    nb = n // B
    vm = pl.BlockSpec(memory_space=pltpu.VMEM)
    dma = pltpu.SemaphoreType.DMA
    f32, bf16 = jnp.float32, jnp.bfloat16
    u, coeffs = pl.pallas_call(
        functools.partial(kernel, n),
        out_shape=[jax.ShapeDtypeStruct((1, 8 * kp), f32), jax.ShapeDtypeStruct((1, nr), f32)],
        in_specs=[pl.BlockSpec(memory_space=pl.ANY), vm, vm, vm],
        out_specs=[vm, vm],
        scratch_shapes=[
            pltpu.VMEM((8, 8, kp), f32),
            pltpu.VMEM((3, PORTIONS, n // 2 + B, H), f32),
            pltpu.VMEM((3, PORTIONS, n // 4, H), f32),
            pltpu.VMEM((3, PORTIONS, n // 4, H), f32),
            pltpu.VMEM((n, kp), bf16),
            pltpu.VMEM((n, kp), bf16),
            pltpu.VMEM((n, kp), bf16),
            pltpu.VMEM((CHUNKS, 2, 2, nr // 2, kp // CHUNKS), bf16),
            pltpu.VMEM((H, nr), f32),
            pltpu.VMEM((8, nr), f32),
            pltpu.VMEM((8, 8, nr), f32),
            pltpu.VMEM((n, n), bf16),
            pltpu.VMEM((n, n), bf16),
            pltpu.VMEM((16, n), f32),
            pltpu.VMEM((nb, B, B), bf16),
            pltpu.VMEM((nb, B, B), bf16),
            pltpu.VMEM((H, H), f32),
            pltpu.VMEM((2, H, H), f32),
            pltpu.VMEM((128, H), f32),
            pltpu.VMEM((16, H), f32),
            pltpu.VMEM((128, H), f32),
            pltpu.VMEM((16, n), f32),
            pltpu.VMEM((16, n), f32),
            dma((CHUNKS, 2)), dma((150,)), dma((150,)), dma((7,)), dma((7,)),
            dma((CHUNKS, 13)), dma((CHUNKS, 13)), dma((CHUNKS,)), dma((7,)), dma((7,)),
        ],
        compiler_params=pltpu.CompilerParams(
            vmem_limit_bytes=58 * 2**20, collective_id=1, has_side_effects=True
        ),
    )(log_derivs, spins.T, hop_energy[None], jnp.asarray(bonds(H), bf16))
    return u.reshape(-1), coeffs.reshape(-1)


def solution(mesh):
    placed = (P("smp", "par"), P("smp", None), P("smp"))
    return jax.shard_map(
        body, mesh=mesh, in_specs=placed, out_specs=(P("par"), P("smp")), check_vma=False
    )
```
